256 devices in a mesh: row: 64 (over y, z, core), node: 4 (over x).
Axes of the slice: x: 4, y: 4, z: 8, core: 2. Of those that a mesh axis runs over, the one named last changes fastest.
Arguments:
- probes: float32 [32, 65536], P(None, 'row'), may hold values from -6 to 6
- diag_blocks: float32 [512, 128, 128], P('row'), may hold values from -0.1875 to 0.1875
- couplings: float32 [512, 3, 128, 128], P('row'), may hold values from -0.1875 to 0.1875
- neighbours: int32 [512, 3], P('row'), may hold values from 0 to 511, as said below
Outputs:
- moments: float32 [16, 32, 65536], P('node', None, 'row')
- projected: float32 [16, 32, 32], P('node')
The draws below stay inside these ranges and needn't reach their ends.
Inputs may be any that keep to these rules, and one draw needn't show every extreme that they name: (neighbours[i, f] - i) modulo 512 lies in 1 to 4, and equals 4 for some entry.
All inputs are finite; a program needn't handle non-finite values.
Results may differ from the reference program's by a relative error of at most 0.0002.
Values sent between devices are 32-bit elements; how exact they have to be, the bound alone decides.
No kernel may reach another device: no remote copies, remote signals or barrier semaphores. Data moves between devices by JAX's collectives and lax.ppermute only.
A program may use at most 64 MiB of HBM per device.

```python
import math
import jax
import jax.numpy as jnp
from jax import lax

BLOCK = 128
PROBES = 32
NODES = 8
MOMENTS = 16
COUPLINGS = 3
REACH = 4
ITERS = 4
BLOCKS = 512
ORDER = 65536


def draw_neighbours(key, part):
    key = jax.random.fold_in(key, 11)
    offsets = jax.random.randint(key, (BLOCKS, COUPLINGS), 1, REACH + 1)
    offsets = offsets.at[BLOCKS - 2, 0].set(1)
    offsets = offsets.at[BLOCKS - 1, 0].set(1)
    offsets = offsets.at[BLOCKS - 1, COUPLINGS - 1].set(REACH)
    positions = jnp.arange(BLOCKS, dtype=jnp.int32)[:, None]
    return ((positions + offsets) % BLOCKS).astype(jnp.int32)


def steps_of(key, extent, shards, smallest, top_value):
    gain, own = 1.0, jax.random.fold_in(key, 6)
    for dim, blocks in shards:
        steps = jnp.exp(jax.random.uniform(jax.random.fold_in(own, dim), (blocks,), jnp.float32, smallest / len(shards), top_value / len(shards)))
        gain = gain * jnp.repeat(steps, extent[dim] // blocks).reshape([-1 if axis == dim else 1 for axis in range(len(extent))])
    return gain


def bell_draw(key, dims, scale, bound, shards=(), kind=jnp.bfloat16):
    values = jax.random.normal(key, dims, jnp.float32) * scale
    if len(shards) > 0:
        values = steps_of(key, dims, shards, -0.22, 0.18) * values
    return jnp.clip(values, min=-bound, max=bound).astype(kind)


def setup_inputs(seed: int = 0) -> dict:
    streams_of = jax.random.split(jax.random.key(seed), 5)
    return {
        "probes": bell_draw(streams_of[0], (PROBES, ORDER), 1.0, 6.0, ((1, 64),), jnp.float32),
        "diag_blocks": bell_draw(streams_of[1], (BLOCKS, BLOCK, BLOCK), (BLOCK * (1 + 2 * COUPLINGS)) ** -0.5, 0.1875, ((0, 64),), jnp.float32),
        "couplings": bell_draw(streams_of[2], (BLOCKS, COUPLINGS, BLOCK, BLOCK), (BLOCK * (1 + 2 * COUPLINGS)) ** -0.5, 0.1875, ((0, 64),), jnp.float32),
        "neighbours": draw_neighbours(jax.random.fold_in(streams_of[4], 71), 0),
    }


highest = lax.Precision.HIGHEST

def reference(probes, diag_blocks, couplings, neighbours):
    block_total = diag_blocks.shape[0]
    block_size = diag_blocks.shape[1]
    probe_count = probes.shape[0]
    symmetric = 0.5 * (diag_blocks + jnp.swapaxes(diag_blocks, 1, 2))
    seeds = probes.reshape(probe_count, block_total, block_size).transpose(1, 0, 2)

    def apply_hamiltonian(vectors):
        gathered = jnp.take(vectors, neighbours, axis=0)
        result = jnp.einsum('bcs,brs->bcr', vectors, symmetric, precision=highest)
        result = result + jnp.einsum('bfcs,bfrs->bcr', gathered, couplings, precision=highest)
        pushed = jnp.einsum('bcr,bfrs->bfcs', vectors, couplings, precision=highest)
        return result.at[neighbours].add(pushed)

    def gram(left, right):
        return jnp.einsum('blr,bmr->lm', left, right, precision=highest)

    def combine(vectors, coeffs):
        return jnp.einsum('blr,lm->bmr', vectors, coeffs, precision=highest)

    def system_solve(matrix, target):
        return jax.scipy.linalg.cho_solve((jnp.linalg.cholesky(matrix), True), target)
    accumulated = jnp.zeros((MOMENTS, block_total, probe_count, block_size), jnp.float32)
    for node in range(NODES):
        angle = math.pi * (node + 0.5) / NODES
        real_shift = math.cos(angle)
        imag_shift = math.sin(angle)

        def shifted(vectors):
            return apply_hamiltonian(vectors) - real_shift * vectors
        solution = jnp.zeros_like(seeds)
        residual = seeds
        direction = seeds
        gram_now = gram(residual, residual)
        for iteration in range(ITERS):
            once = shifted(direction)
            image = shifted(once) + imag_shift * imag_shift * direction
            alpha = system_solve(gram(direction, image), gram_now)
            solution = solution + combine(direction, alpha)
            if iteration + 1 < ITERS:
                residual = residual - combine(image, alpha)
                gram_next = gram(residual, residual)
                beta = system_solve(gram_now, gram_next)
                direction = residual + combine(direction, beta)
                gram_now = gram_next
        applied = shifted(solution)
        orders = jnp.arange(MOMENTS, dtype=jnp.float32) + 1.0
        weight_real = jnp.cos(orders * angle) / 8.0
        weight_imag = jnp.sin(orders * angle) * imag_shift / 8.0
        accumulated = accumulated + weight_imag[:, None, None, None] * solution[None] - weight_real[:, None, None, None] * applied[None]
    moments = accumulated.transpose(0, 2, 1, 3).reshape(MOMENTS, probe_count, block_total * block_size)
    projected = jnp.einsum('lr,kmr->klm', probes, moments, precision=highest) / (block_total * block_size)
    return (moments, projected)
```

```python
import functools
import math

import jax
import jax.numpy as jnp
import numpy as np
from jax import lax
from jax.experimental import pallas as pl
from jax.experimental.pallas import tpu as pltpu
from jax.sharding import PartitionSpec as P

NODES = 8
MOMENTS = 16
REACH = 4
ITERS = 4
PROBES = 32
BLOCK = 128
ROWS = 1024
HALF = 512
TILE = 256
DEGREE = 2 * ITERS - 1
BLOCKS = 512
ORDER_DIM = BLOCKS * BLOCK
SCALE = 16.0

f32 = jnp.float32
bf16 = jnp.bfloat16
highest = lax.Precision.HIGHEST

VMEM = pl.BlockSpec(memory_space=pltpu.VMEM)
SMEM = pl.BlockSpec(memory_space=pltpu.SMEM)


HBM = pl.BlockSpec(memory_space=pltpu.HBM)


def call(body, outs, in_specs, flops=0, bytes_accessed=0, vmem=8, scratch=()):
    return pl.pallas_call(
        body,
        out_shape=outs,
        in_specs=in_specs,
        out_specs=jax.tree.map(lambda _: VMEM, outs),
        scratch_shapes=scratch,
        compiler_params=pltpu.CompilerParams(vmem_limit_bytes=vmem << 20),
        cost_estimate=pl.CostEstimate(flops=flops, bytes_accessed=bytes_accessed, transcendentals=0),
    )


def halves(value):
    high = value.astype(bf16)
    return high, (value - high.astype(f32)).astype(bf16)


def stacked(value):
    high, low = halves(value)
    return jnp.concatenate([high, low], axis=0)


def dot_nn(left, right):
    return lax.dot_general(left, right, (((1,), (0,)), ((), ())), preferred_element_type=f32)


def dot_nt(left, right):
    return lax.dot_general(left, right, (((1,), (1,)), ((), ())), preferred_element_type=f32)


def fold(double):
    return double[:PROBES] + double[PROBES:]


def product(dot, pair, high, low):
    return fold(dot(pair, high)) + dot(pair[:PROBES], low)


def payloads(parity, near, spill, pay_core, pay_chip):
    even = parity == 0
    pay_core[...] = jnp.where(even, spill, near)
    pay_chip[...] = jnp.where(even, near, spill)


def cross_out(tail, uhi, ulo):
    pair = stacked(tail)
    first = product(dot_nn, pair, uhi[:, :TILE], ulo[:, :TILE])
    second = product(dot_nn, pair[:, TILE:], uhi[TILE:, TILE:], ulo[TILE:, TILE:])
    return jnp.concatenate([first, second], axis=1)


def cross_in(ahead, uhi, ulo):
    pair = stacked(ahead)
    first = product(dot_nt, pair[:, :TILE], uhi[:TILE, :TILE], ulo[:TILE, :TILE])
    second = product(dot_nt, pair, uhi[TILE:, :], ulo[TILE:, :])
    return jnp.concatenate([first, second], axis=1)


def band_block(step, row, neighbours, position, diag, coup):
    if step == 0:
        return diag * (0.5 / SCALE)
    block = jnp.zeros((BLOCK, BLOCK), f32)
    for f in range(neighbours.shape[0]):
        distance = (neighbours[f, row] - (position * 8 + row)) & (BLOCKS - 1)
        block = block + jnp.where(distance == step, coup[f], 0.0)
    return block * (1.0 / SCALE)


def cross_rows(i, neighbours, position, coup, uhi, ulo):
    zero = jnp.zeros((BLOCK, BLOCK), bf16)
    rows = pl.ds((i - 4) * BLOCK, BLOCK)
    for col in range(4):
        cols = pl.ds(col * BLOCK, BLOCK)
        if i + REACH < 8 + col:
            uhi[rows, cols] = zero
            ulo[rows, cols] = zero
        else:
            block = band_block(8 + col - i, i, neighbours, position, None, coup)
            uhi[rows, cols], ulo[rows, cols] = halves(block)


def cross_body(neighbours, position, coup_hbm, x_hbm, pay_core, pay_chip, coup, x, uhi, ulo, sems):
    copies = [pltpu.make_async_copy(coup_hbm.at[i], coup.at[i - 4], sems.at[i - 4]) for i in (7, 6, 5, 4)]
    for copy in copies:
        copy.start()
    load = pltpu.make_async_copy(x_hbm, x, sems.at[4])
    load.start()
    for i, copy in zip((7, 6, 5, 4), copies):
        copy.wait()
        cross_rows(i, neighbours, position[0], coup.at[i - 4], uhi, ulo)
    load.wait()
    payloads(position[0] & 1, x[:, :HALF], cross_out(x[:, HALF:], uhi, ulo), pay_core, pay_chip)


def gram_of(x, before):
    both = jnp.concatenate([before, x], axis=0)
    return lax.dot_general(x, both, (((1,), (1,)), ((), ())), precision=highest, preferred_element_type=f32)


def first_body(neighbours, position, diag, coup, x, thi, tlo, uhi, ulo, local, gram):
    zero = jnp.zeros((BLOCK, BLOCK), bf16)
    for i in range(8):
        tile, part = divmod(i, 2)
        rows = pl.ds(part * BLOCK, BLOCK)
        for col in range(min(6, 8 - 2 * tile)):
            cols = pl.ds(col * BLOCK, BLOCK)
            step = col - part
            if 0 <= step <= REACH:
                block = band_block(step, i, neighbours, position[0], diag[i] if step == 0 else None, coup.at[i])
                thi[tile, rows, cols], tlo[tile, rows, cols] = halves(block)
            else:
                thi[tile, rows, cols] = zero
                tlo[tile, rows, cols] = zero
        if i >= 4:
            cross_rows(i, neighbours, position[0], coup.at[i], uhi, ulo)
    local_body(x, x, thi, tlo, local, gram)


def local_body(x, before, thi, tlo, local, gram):
    value = x[...]
    gram[...] = gram_of(value, before[...])
    pair = stacked(value)
    wide = [jnp.zeros((2 * PROBES, TILE), f32) for _ in range(4)]
    thin = [jnp.zeros((PROBES, TILE), f32) for _ in range(4)]
    for row in range(4):
        for col in range(row, min(row + 3, 4)):
            at = slice((col - row) * TILE, (col - row + 1) * TILE)
            high, low = thi[row, :, at], tlo[row, :, at]
            from_row, from_col = pair[:, row * TILE:(row + 1) * TILE], pair[:, col * TILE:(col + 1) * TILE]
            wide[col] = wide[col] + dot_nn(from_row, high)
            thin[col] = thin[col] + dot_nn(from_row[:PROBES], low)
            wide[row] = wide[row] + dot_nt(from_col, high)
            thin[row] = thin[row] + dot_nt(from_col[:PROBES], low)
    for tile in range(4):
        local[:, tile * TILE:(tile + 1) * TILE] = fold(wide[tile]) + thin[tile]


def join_body(parity, local, got_core, got_chip, uhi, ulo, out, *pay):
    even = parity[0] & 1 == 0
    ahead = jnp.where(even, got_core[...], got_chip[...])
    arrived = jnp.where(even, got_chip[...], got_core[...])
    near = local[:, :HALF] + arrived
    tail = local[:, HALF:] + cross_in(ahead, uhi, ulo)
    out[:, :HALF] = near
    out[:, HALF:] = tail
    if pay:
        payloads(parity[0] & 1, near, cross_out(tail, uhi, ulo), *pay)


def last_gram_body(x, before, gram):
    gram[...] = gram_of(x[...], before[...])


def dot_f32(left, right):
    return lax.dot_general(left, right, (((1,), (0,)), ((), ())), precision=highest, preferred_element_type=f32)


WIDTH = NODES * PROBES
PANEL = 8


def invert(matrix):
    rows = lax.broadcasted_iota(jnp.int32, (PROBES, WIDTH), 0)
    lanes = lax.broadcasted_iota(jnp.int32, (PROBES, WIDTH), 1) % PROBES
    group = lax.broadcasted_iota(jnp.int32, (PROBES, BLOCK), 1) // PROBES * PROBES
    for start in range(0, PROBES, PANEL):
        columns = [
            jnp.concatenate(
                [jnp.take_along_axis(matrix[:, h:h + BLOCK], group + k, axis=1) for h in range(0, WIDTH, BLOCK)], axis=1
            )
            for k in range(start, start + PANEL)
        ]
        for m in range(PANEL):
            k = start + m
            on_row, on_lane = rows == k, lanes == k
            inverse = 1.0 / columns[m][k:k + 1]
            factor = jnp.where(on_row, -1.0, columns[m])
            scaled = jnp.where(on_lane[:1], 1.0, matrix[k:k + 1]) * inverse
            matrix = jnp.where(on_lane | on_row, 0.0, matrix) - factor * scaled
            for q in range(m + 1, PANEL):
                columns[q] = jnp.where(on_row, 0.0, columns[q]) - factor * (columns[q][k:k + 1] * inverse)
    return matrix


def node_diagonal():
    return (
        lax.broadcasted_iota(jnp.int32, (WIDTH, WIDTH), 0) // PROBES
        == lax.broadcasted_iota(jnp.int32, (WIDTH, WIDTH), 1) // PROBES
    )


def node_shifts():
    node = lax.broadcasted_iota(jnp.int32, (1, WIDTH), 1) // PROBES
    cosine = jnp.zeros((1, WIDTH), f32)
    square = jnp.zeros((1, WIDTH), f32)
    for j in range(NODES):
        angle = math.pi * (j + 0.5) / NODES
        cosine = jnp.where(node == j, np.float32(math.cos(angle)), cosine)
        square = jnp.where(node == j, np.float32(math.sin(angle) ** 2), square)
    return cosine, square


def grown(coeffs, blocks=1):
    return jnp.concatenate([coeffs, jnp.zeros((blocks * PROBES, WIDTH), f32)], axis=0)


def sunk(coeffs, cosine):
    below = jnp.concatenate([jnp.zeros((PROBES, WIDTH), f32), coeffs], axis=0)
    return SCALE * below - cosine * grown(coeffs)


def raised(against, cosine):
    return SCALE * against[PROBES:] - cosine * against[:-PROBES]


class Nodes:
    def __init__(self):
        self.diagonal = node_diagonal()
        self.cosine, self.square = node_shifts()

    def blocks(self, full):
        masked = jnp.where(self.diagonal, full, 0.0)
        return sum(masked[j * PROBES:(j + 1) * PROBES] for j in range(NODES))

    def spread(self, matrix):
        return jnp.where(self.diagonal, jnp.concatenate([matrix] * NODES, axis=0), 0.0)

    def inner(self, left, against):
        return self.blocks(dot_f32(left.T, against[:left.shape[0]]))

    def image(self, direction, dir_against):
        once, once_against = sunk(direction, self.cosine), raised(dir_against, self.cosine)
        image = sunk(once, self.cosine) + self.square * grown(direction, 2)
        image_against = raised(once_against, self.cosine) + self.square * dir_against[:-2 * PROBES]
        return image, image_against

    def step(self, state, last):
        direction, residual, dir_against, res_against, solution = state
        size = direction.shape[0]
        image, image_against = self.image(direction, dir_against)
        if size == PROBES:
            curvature, now = image_against[:size], res_against[:size]
        else:
            turned = direction.T
            curvature = self.blocks(dot_f32(turned, image_against[:size]))
            now = self.blocks(dot_f32(turned, res_against[:size]))
        inverse = invert(curvature)
        alpha = self.spread(dot_f32(inverse, self.spread(now)))
        if last:
            return grown(solution, 2) + dot_f32(direction, alpha)
        moved = dot_f32(jnp.concatenate([direction, image, image_against], axis=0), alpha)
        part = size + image.shape[0]
        solution = moved[:size] if solution is None else grown(solution, 2) + moved[:size]
        residual = grown(residual, 2) - moved[size:part]
        res_against = res_against[:-2 * PROBES] - moved[part:]
        beta = self.spread(dot_f32(inverse, self.spread(self.inner(image, res_against))))
        count = res_against.shape[0]
        moved = dot_f32(jnp.concatenate([direction, dir_against[:count]], axis=0), beta)
        direction = residual - grown(moved[:size], 2)
        dir_against = res_against - moved[size:]
        return direction, residual, dir_against, res_against, solution


def moment_coeffs(nodes, weights, first, share, solution):
    applied = sunk(solution, nodes.cosine)
    row = lax.broadcasted_iota(jnp.int32, (PROBES, share * PROBES), 0)
    lane = lax.broadcasted_iota(jnp.int32, (PROBES, share * PROBES), 1)
    imag, real = [], []
    for j in range(NODES):
        for part, (table, sign) in ((imag, (0, 1.0)), (real, (1, -1.0))):
            block = jnp.zeros((PROBES, share * PROBES), f32)
            for k in range(share):
                block = jnp.where(lane == row + k * PROBES, sign * weights[table, first + k, j], block)
            part.append(block)
    left = jnp.concatenate([grown(solution), applied], axis=1)
    return dot_f32(left, jnp.concatenate(imag + real, axis=0))


def moments_body(node, weights, gram, k0, k1, k2, k3, k4, k5, k6, k7, moments, projected):
    nodes = Nodes()
    count = 2 * DEGREE + 1
    against = jnp.concatenate(
        [jnp.concatenate([gram[:, (a + 1) * PROBES:(a + 2) * PROBES]] * NODES, axis=1) for a in range(count)], axis=0
    )
    eye = (
        lax.broadcasted_iota(jnp.int32, (PROBES, WIDTH), 0)
        == lax.broadcasted_iota(jnp.int32, (PROBES, WIDTH), 1) % PROBES
    ).astype(f32)
    state = (eye, eye, against, against, None)
    for iteration in range(ITERS):
        state = nodes.step(state, iteration + 1 == ITERS)
    share = moments.shape[0]
    coeffs = moment_coeffs(nodes, weights, node[0] * share, share, state)
    basis = jnp.concatenate([k[...] for k in (k0, k1, k2, k3, k4, k5, k6, k7)], axis=0)
    moments[...] = dot_f32(coeffs.T, basis).reshape(share, PROBES, ROWS)
    onto = dot_f32(gram[:, PROBES:PROBES * (DEGREE + 2)], coeffs) * (1.0 / ORDER_DIM)
    for k in range(share):
        projected[k] = onto[:, k * PROBES:(k + 1) * PROBES]


def exchange(value, partner):
    count = lax.axis_size("row")
    return lax.ppermute(value, "row", [(source, partner(source) % count) for source in range(count)])


def core_partner(i):
    return i ^ 1


def chip_partner(i):
    return i + 1 if i % 2 else i - 1


def ring_partner(stage, i):
    y, z, core = i // 16, i // 2 % 8, i % 2
    if stage < 3:
        z = (z ^ 1, z ^ 2, (6, 7, 4, 5, 2, 3, 0, 1)[z])[stage]
    else:
        y = (y ^ 1, y ^ 3)[stage - 3]
    return y * 16 + z * 2 + core


def reduce_rows(value, parity):
    half = value.shape[0] // 2
    mine = lax.dynamic_slice_in_dim(value, parity * half, half, 0)
    other = lax.dynamic_slice_in_dim(value, (1 - parity) * half, half, 0)
    mine = mine + exchange(other, core_partner)
    for stage in range(5):
        mine = mine + exchange(mine, functools.partial(ring_partner, stage))
    other = exchange(mine, core_partner)
    first = jnp.where(parity == 0, mine, other)
    second = jnp.where(parity == 0, other, mine)
    return jnp.concatenate([first, second], axis=0)


def moment_weights():
    orders = np.arange(MOMENTS)[:, None] + 1.0
    angles = np.pi * (np.arange(NODES)[None, :] + 0.5) / NODES
    imag = np.sin(orders * angles) * np.sin(angles) / 8.0
    real = np.cos(orders * angles) / 8.0
    return np.stack([imag, real]).astype(np.float32)


def shards(probes, diag_blocks, couplings, neighbours):
    moment_share = MOMENTS // lax.axis_size("node")
    position = lax.axis_index("row")
    parity = position % 2
    flag = position.reshape(1)
    node = lax.axis_index("node").reshape(1)
    near_by = neighbours.T
    def array(*shape, kind=f32):
        return jax.ShapeDtypeStruct(shape, kind)

    message = array(PROBES, HALF)
    cross = (array(HALF, HALF, kind=bf16),) * 2
    pay_core, pay_chip = call(
        cross_body,
        (message, message),
        [SMEM, SMEM, HBM, HBM],
        vmem=56,
        scratch=[
            pltpu.VMEM((4, 3, BLOCK, BLOCK), f32),
            pltpu.VMEM((PROBES, ROWS), f32),
            pltpu.VMEM((HALF, HALF), bf16),
            pltpu.VMEM((HALF, HALF), bf16),
            pltpu.SemaphoreType.DMA((5,)),
        ],
    )(near_by, flag, couplings, probes)
    vector = array(PROBES, ROWS)
    pair = array(PROBES, 2 * PROBES)
    basis = [probes]
    grams = []
    for degree in range(DEGREE):
        got_core = exchange(pay_core, core_partner)
        got_chip = exchange(pay_chip, chip_partner)
        if degree == 0:
            thi, tlo, uhi, ulo, local, gram = call(
                first_body,
                (array(4, TILE, 3 * TILE, kind=bf16),) * 2 + cross + (vector, pair),
                [SMEM, SMEM, VMEM, VMEM, VMEM],
                flops=10**9,
                bytes_accessed=4 << 20,
                vmem=16,
            )(near_by, flag, diag_blocks, couplings, probes)
        else:
            local, gram = call(local_body, (vector, pair), [VMEM] * 4, flops=10**9, bytes_accessed=4 << 20)(
                basis[-1], basis[-2], thi, tlo
            )
        grams.append(gram)
        more = degree + 1 < DEGREE
        value, *pay = call(
            join_body,
            (vector, message, message) if more else (vector,),
            [SMEM] + [VMEM] * 5,
            flops=10**8,
            bytes_accessed=2 << 20,
        )(flag, local, got_core, got_chip, uhi, ulo)
        if more:
            pay_core, pay_chip = pay
        basis.append(value)
    grams.append(call(last_gram_body, array(PROBES, 2 * PROBES), [VMEM] * 2)(basis[-1], basis[-2]))
    total = reduce_rows(jnp.concatenate(grams, axis=1), parity)
    moments, projected = call(
        moments_body,
        (array(moment_share, PROBES, ROWS), array(moment_share, PROBES, PROBES)),
        [SMEM, SMEM] + [VMEM] * 9,
        vmem=24,
    )(node, jnp.asarray(moment_weights()), total, *basis)
    return (moments, projected)


def solution(mesh):
    placed = (P(None, "row"), P("row", None, None), P("row", None, None, None), P("row", None))
    return jax.shard_map(
        shards,
        mesh=mesh,
        in_specs=placed,
        out_specs=(P("node", None, "row"), P("node", None, None)),
        check_vma=False,
    )
```

```python
import functools
import math

import jax
import jax.numpy as jnp
import numpy as np
from jax import lax
from jax.experimental import pallas as pl
from jax.experimental.pallas import tpu as pltpu
from jax.sharding import PartitionSpec as P

NODES = 8
MOMENTS = 16
REACH = 4
ITERS = 4
PROBES = 32
BLOCK = 128
ROWS = 1024
HALF = 512
TILE = 256
DEGREE = 2 * ITERS - 1
BLOCKS = 512
ORDER_DIM = BLOCKS * BLOCK
SCALE = 16.0

f32 = jnp.float32
bf16 = jnp.bfloat16
highest = lax.Precision.HIGHEST

TILES = [(row, col) for row in range(4) for col in range(row, min(row + 3, 4))]
EDGE = [(row, col) for row in range(REACH) for col in range(row + 1)]

VMEM = pl.BlockSpec(memory_space=pltpu.VMEM)
SMEM = pl.BlockSpec(memory_space=pltpu.SMEM)


HBM = pl.BlockSpec(memory_space=pltpu.HBM)


def call(body, outs, in_specs, flops=0, bytes_accessed=0, vmem=8, scratch=(), out_specs=None, aliases=()):
    return pl.pallas_call(
        body,
        out_shape=outs,
        in_specs=in_specs,
        out_specs=jax.tree.map(lambda _: VMEM, outs) if out_specs is None else out_specs,
        input_output_aliases=dict(aliases),
        scratch_shapes=scratch,
        compiler_params=pltpu.CompilerParams(vmem_limit_bytes=vmem << 20),
        cost_estimate=pl.CostEstimate(flops=flops, bytes_accessed=bytes_accessed, transcendentals=0),
    )


def halves(value):
    high = value.astype(bf16)
    return high, (value - high.astype(f32)).astype(bf16)


def stacked(value):
    high, low = halves(value)
    return jnp.concatenate([high, low], axis=0)


def dot_nn(left, right):
    return lax.dot_general(left, right, (((1,), (0,)), ((), ())), preferred_element_type=f32)


def dot_nt(left, right):
    return lax.dot_general(left, right, (((1,), (1,)), ((), ())), preferred_element_type=f32)


def fold(double):
    half = double.shape[0] // 2
    return double[:half] + double[half:]


def product(dot, pair, high, low):
    return fold(dot(pair, high)) + dot(pair[:pair.shape[0] // 2], low)


def payloads(parity, near, spill, pay_core, pay_chip):
    even = parity == 0
    pay_core[...] = jnp.where(even, spill, near)
    pay_chip[...] = jnp.where(even, near, spill)


def cross_out(tail, uhi, ulo):
    pair = stacked(tail)
    left, right = pair[:, :TILE], pair[:, TILE:]
    first = product(dot_nn, left, uhi[0], ulo[0]) + product(dot_nn, right, uhi[1], ulo[1])
    return jnp.concatenate([first, product(dot_nn, right, uhi[2], ulo[2])], axis=1)


def cross_in(ahead, uhi, ulo):
    pair = stacked(ahead)
    left, right = pair[:, :TILE], pair[:, TILE:]
    second = product(dot_nt, left, uhi[1], ulo[1]) + product(dot_nt, right, uhi[2], ulo[2])
    return jnp.concatenate([product(dot_nt, left, uhi[0], ulo[0]), second], axis=1)


def band_block(step, row, neighbours, position, diag, coup):
    if step == 0:
        return diag * (0.5 / SCALE)
    block = jnp.zeros((BLOCK, BLOCK), f32)
    for f in range(neighbours.shape[0]):
        distance = (neighbours[f, row] - (position * 8 + row)) & (BLOCKS - 1)
        block = block + jnp.where(distance == step, coup[f], 0.0)
    return block * (1.0 / SCALE)


def cross_place(row, col):
    return row // 2 + col // 2, pl.ds(row % 2 * BLOCK, BLOCK), pl.ds(col % 2 * BLOCK, BLOCK)


def cross_zero(uhi, ulo):
    zero = jnp.zeros((BLOCK, BLOCK), bf16)
    for row, col in ((0, 1), (2, 3)):
        uhi[cross_place(row, col)] = zero
        ulo[cross_place(row, col)] = zero


def cross_rows(i, neighbours, position, coup, uhi, ulo, edge=None):
    row = i - 4
    for col in range(row + 1):
        block = band_block(8 + col - i, i, neighbours, position, None, coup)
        uhi[cross_place(row, col)], ulo[cross_place(row, col)] = halves(block)
        if edge is not None:
            edge[EDGE.index((row, col))] = block


def cross_body(neighbours, position, coup_hbm, x_hbm, pay_core, pay_chip, coup, x, uhi, ulo, sems):
    copies = [pltpu.make_async_copy(coup_hbm.at[i], coup.at[i - 4], sems.at[i - 4]) for i in (7, 6, 5, 4)]
    for copy in copies:
        copy.start()
    load = pltpu.make_async_copy(x_hbm, x, sems.at[4])
    load.start()
    cross_zero(uhi, ulo)
    for i, copy in zip((7, 6, 5, 4), copies):
        copy.wait()
        cross_rows(i, neighbours, position[0], coup.at[i - 4], uhi, ulo)
    load.wait()
    payloads(position[0] & 1, x[:, :HALF], cross_out(x[:, HALF:], uhi, ulo), pay_core, pay_chip)


def gram_of(x, before):
    both = jnp.concatenate([before, x], axis=0)
    return lax.dot_general(x, both, (((1,), (1,)), ((), ())), precision=highest, preferred_element_type=f32)


def first_body(neighbours, position, diag, coup, x, after, thi, tlo, uhi, ulo, edge, local, gram):
    zero = jnp.zeros((BLOCK, BLOCK), bf16)
    for tile, (row, col) in enumerate(TILES):
        for up in range(2):
            for across in range(2):
                i, step = 2 * row + up, 2 * (col - row) + across - up
                at = tile, pl.ds(up * BLOCK, BLOCK), pl.ds(across * BLOCK, BLOCK)
                if 0 <= step <= REACH:
                    block = band_block(step, i, neighbours, position[0], diag[i] if step == 0 else None, coup.at[i])
                    thi[at], tlo[at] = halves(block)
                else:
                    thi[at] = zero
                    tlo[at] = zero
    cross_zero(uhi, ulo)
    for i in range(4, 8):
        cross_rows(i, neighbours, position[0], coup.at[i], uhi, ulo, edge)
    value = x[...]
    local[...] = times_local(value, thi, tlo)
    gram[...] = gram_of(value, value)


def times_local(value, thi, tlo):
    pair = stacked(value)
    wide = [jnp.zeros((2 * PROBES, TILE), f32) for _ in range(4)]
    thin = [jnp.zeros((PROBES, TILE), f32) for _ in range(4)]
    for tile, (row, col) in enumerate(TILES):
        high, low = thi[tile], tlo[tile]
        from_row, from_col = pair[:, row * TILE:(row + 1) * TILE], pair[:, col * TILE:(col + 1) * TILE]
        wide[col] = wide[col] + dot_nn(from_row, high)
        thin[col] = thin[col] + dot_nn(from_row[:PROBES], low)
        wide[row] = wide[row] + dot_nt(from_col, high)
        thin[row] = thin[row] + dot_nt(from_col[:PROBES], low)
    return jnp.concatenate([fold(w) + t for w, t in zip(wide, thin)], axis=1)


def joined(local, arrived, inward):
    return jnp.concatenate([local[:, :HALF] + arrived, local[:, HALF:] + inward], axis=1)


def send_two(position, value, thi, tlo, uhi, ulo, local, spill, pay_core, pay_chip):
    following = times_local(value, thi, tlo)
    local[...] = following
    both = cross_out(jnp.concatenate([value[:, HALF:], following[:, HALF:]], axis=0), uhi, ulo)
    spill[...] = both[:PROBES]
    near = jnp.concatenate([value[:, :HALF], following[:, :HALF]], axis=0)
    payloads(position[0] & 1, near, both, pay_core, pay_chip)


def received(position, got_core, got_chip):
    even = position[0] & 1 == 0
    core, chip = got_core[...], got_chip[...]
    return jnp.where(even, core, chip), jnp.where(even, chip, core)


def start_body(position, local, got_core, got_chip, thi, tlo, uhi, ulo, kept, out, *rest):
    *sent, sems = rest
    ahead, arrived = received(position, got_core, got_chip)
    value = joined(local, arrived, cross_in(ahead, uhi, ulo))
    out[...] = value
    keep = pltpu.make_async_copy(out, kept.at[1], sems.at[0])
    keep.start()
    send_two(position, value, thi, tlo, uhi, ulo, *sent)
    keep.wait()


def double_body(
    kept_in, position, before, local, spill, correction, got_core, got_chip, thi, tlo, uhi, ulo, kept, first, second, *rest,
    degree
):
    *sent, sems = rest
    ahead, arrived = received(position, got_core, got_chip)
    ahead = jnp.concatenate([ahead[:PROBES], ahead[PROBES:] + spill[...]], axis=0)
    inward = cross_in(ahead, uhi, ulo)
    value = joined(local, arrived[:PROBES], inward[:PROBES])
    first[...] = value
    keeps = [pltpu.make_async_copy(ref, kept.at[degree + 1 + n], sems.at[n]) for n, ref in enumerate((first, second))]
    keeps[0].start()
    local = times_local(value, thi, tlo)
    after = joined(local, arrived[PROBES:] + correction[...], inward[PROBES:])
    second[...] = after
    keeps[1].start()
    if len(sent) > 2:
        send_two(position, after, thi, tlo, uhi, ulo, *sent)
    else:
        sums = jnp.concatenate([gram_of(value, before[...]), gram_of(after, value)], axis=1)
        store_halves(position, sums, *sent)
    for keep in keeps:
        keep.wait()


def store_halves(position, sums, mine, other):
    upper, lower = sums[:PROBES // 2], sums[PROBES // 2:]
    even = position[0] & 1 == 0
    mine[...] = jnp.where(even, upper, lower)
    other[...] = jnp.where(even, lower, upper)


def shadow_body(position, *refs, count, first, last):
    vectors, (done, up_hi, up_lo), outs = refs[:count], refs[count:count + 3], refs[count + 3:]
    correction, outs = outs[0], outs[1:]
    if first:
        phi, plo = outs[1:]
        cross_zero(phi, plo)
        for n, (row, col) in enumerate(EDGE):
            phi[cross_place(row, col)], plo[cross_place(row, col)] = halves(up_hi[n])
    else:
        phi, plo = up_hi, up_lo
    sums = [done[...]] + [gram_of(vectors[n][...], vectors[n - 1][...]) for n in range(1, count)]
    sums = jnp.concatenate(sums, axis=1)
    if last:
        store_halves(position, sums, *outs)
    else:
        outs[0][...] = sums
    correction[...] = cross_out(cross_in(vectors[-1][:, :HALF], phi, plo), phi, plo)


def dot_f32(left, right):
    return lax.dot_general(left, right, (((1,), (0,)), ((), ())), precision=highest, preferred_element_type=f32)


WIDTH = NODES * PROBES
PANEL = 8


def invert(matrix):
    rows = lax.broadcasted_iota(jnp.int32, (PROBES, WIDTH), 0)
    lanes = lax.broadcasted_iota(jnp.int32, (PROBES, WIDTH), 1) % PROBES
    group = lax.broadcasted_iota(jnp.int32, (PROBES, BLOCK), 1) // PROBES * PROBES
    for start in range(0, PROBES, PANEL):
        columns = [
            jnp.concatenate(
                [jnp.take_along_axis(matrix[:, h:h + BLOCK], group + k, axis=1) for h in range(0, WIDTH, BLOCK)], axis=1
            )
            for k in range(start, start + PANEL)
        ]
        for m in range(PANEL):
            k = start + m
            on_row, on_lane = rows == k, lanes == k
            inverse = 1.0 / columns[m][k:k + 1]
            factor = jnp.where(on_row, -1.0, columns[m])
            scaled = jnp.where(on_lane[:1], 1.0, matrix[k:k + 1]) * inverse
            matrix = jnp.where(on_lane | on_row, 0.0, matrix) - factor * scaled
            for q in range(m + 1, PANEL):
                columns[q] = jnp.where(on_row, 0.0, columns[q]) - factor * (columns[q][k:k + 1] * inverse)
    return matrix


def node_diagonal():
    return (
        lax.broadcasted_iota(jnp.int32, (WIDTH, WIDTH), 0) // PROBES
        == lax.broadcasted_iota(jnp.int32, (WIDTH, WIDTH), 1) // PROBES
    )


def node_shifts():
    node = lax.broadcasted_iota(jnp.int32, (1, WIDTH), 1) // PROBES
    cosine = jnp.zeros((1, WIDTH), f32)
    square = jnp.zeros((1, WIDTH), f32)
    for j in range(NODES):
        angle = math.pi * (j + 0.5) / NODES
        cosine = jnp.where(node == j, np.float32(math.cos(angle)), cosine)
        square = jnp.where(node == j, np.float32(math.sin(angle) ** 2), square)
    return cosine, square


def grown(coeffs, blocks=1):
    return jnp.concatenate([coeffs, jnp.zeros((blocks * PROBES, WIDTH), f32)], axis=0)


def sunk(coeffs, cosine):
    below = jnp.concatenate([jnp.zeros((PROBES, WIDTH), f32), coeffs], axis=0)
    return SCALE * below - cosine * grown(coeffs)


def raised(against, cosine):
    return SCALE * against[PROBES:] - cosine * against[:-PROBES]


class Nodes:
    def __init__(self):
        self.diagonal = node_diagonal()
        self.cosine, self.square = node_shifts()

    def blocks(self, full):
        masked = jnp.where(self.diagonal, full, 0.0)
        return sum(masked[j * PROBES:(j + 1) * PROBES] for j in range(NODES))

    def spread(self, matrix):
        return jnp.where(self.diagonal, jnp.concatenate([matrix] * NODES, axis=0), 0.0)

    def inner(self, left, against):
        return self.blocks(dot_f32(left.T, against[:left.shape[0]]))

    def image(self, direction, dir_against):
        once, once_against = sunk(direction, self.cosine), raised(dir_against, self.cosine)
        image = sunk(once, self.cosine) + self.square * grown(direction, 2)
        image_against = raised(once_against, self.cosine) + self.square * dir_against[:-2 * PROBES]
        return image, image_against

    def alpha(self, direction, residual, dir_against, res_against, solution):
        size = direction.shape[0]
        image, image_against = self.image(direction, dir_against)
        if size == PROBES:
            curvature, now = image_against[:size], res_against[:size]
        else:
            turned = direction.T
            curvature = self.blocks(dot_f32(turned, image_against[:size]))
            now = self.blocks(dot_f32(turned, res_against[:size]))
        inverse = invert(curvature)
        alpha = self.spread(dot_f32(inverse, self.spread(now)))
        if residual is None:
            return grown(solution, 2) + dot_f32(direction, alpha)
        moved = dot_f32(jnp.concatenate([direction, image, image_against], axis=0), alpha)
        part = size + image.shape[0]
        solution = moved[:size] if solution is None else grown(solution, 2) + moved[:size]
        residual = grown(residual, 2) - moved[size:part]
        res_against = res_against[:-2 * PROBES] - moved[part:]
        return image, inverse, residual, res_against, solution

    def beta(self, direction, dir_against, image, inverse, residual, res_against):
        size, count = direction.shape[0], res_against.shape[0]
        beta = self.spread(dot_f32(inverse, self.spread(self.inner(image, res_against))))
        moved = dot_f32(jnp.concatenate([direction, dir_against[:count]], axis=0), beta)
        return residual - grown(moved[:size], 2), res_against - moved[size:]


def moment_coeffs(nodes, weights, first, share, solution):
    applied = sunk(solution, nodes.cosine)
    row = lax.broadcasted_iota(jnp.int32, (PROBES, share * PROBES), 0)
    lane = lax.broadcasted_iota(jnp.int32, (PROBES, share * PROBES), 1)
    imag, real = [], []
    for j in range(NODES):
        for part, (table, sign) in ((imag, (0, 1.0)), (real, (1, -1.0))):
            block = jnp.zeros((PROBES, share * PROBES), f32)
            for k in range(share):
                block = jnp.where(lane == row + k * PROBES, sign * weights[table, first + k, j], block)
            part.append(block)
    left = jnp.concatenate([grown(solution), applied], axis=1)
    return dot_f32(left, jnp.concatenate(imag + real, axis=0))


def whole(position, mine, other):
    even = position[0] & 1 == 0
    upper, lower = jnp.where(even, mine[...], other[...]), jnp.where(even, other[...], mine[...])
    return jnp.concatenate([upper, lower], axis=0)


def store(outs, values):
    for out, value in zip(outs, values):
        out[...] = value


def zeroth_body(position, mine, other, *outs):
    nodes = Nodes()
    sums = whole(position, mine, other)
    against = jnp.concatenate(
        [
            jnp.concatenate([sums[:, at:at + PROBES]] * NODES, axis=1)
            for at in range(PROBES, sums.shape[1], PROBES)
        ],
        axis=0,
    )
    eye = (
        lax.broadcasted_iota(jnp.int32, (PROBES, WIDTH), 0)
        == lax.broadcasted_iota(jnp.int32, (PROBES, WIDTH), 1) % PROBES
    ).astype(f32)
    image, inverse, residual, res_against, solution = nodes.alpha(eye, eye, against, against, None)
    direction, dir_against = nodes.beta(eye, against, image, inverse, residual, res_against)
    store(outs, (direction, residual, dir_against, res_against, solution))


def iterate_body(*refs):
    nodes = Nodes()
    direction, residual, dir_against, res_against, solution = (ref[...] for ref in refs[:5])
    image, inverse, residual, res_against, solution = nodes.alpha(
        direction, residual, dir_against, res_against, solution
    )
    direction, dir_against = nodes.beta(direction, dir_against, image, inverse, residual, res_against)
    store(refs[5:], (direction, residual, dir_against, res_against, solution))


def alpha_body(*refs):
    store(refs[5:], Nodes().alpha(*(ref[...] for ref in refs[:5])))


def moments_body(
    node, position, weights, mine, other, mine_late, other_late, direction, dir_against,
    image, inverse, residual, res_against, solution, k0, kept, moments, projected, basis, sems
):
    loads = [pltpu.make_async_copy(k0, basis.at[0], sems.at[0])]
    loads += [pltpu.make_async_copy(kept.at[d], basis.at[d], sems.at[d]) for d in range(1, DEGREE + 1)]
    for load in loads:
        load.start()
    nodes = Nodes()
    sums = jnp.concatenate([whole(position, mine, other)[:, PROBES:], whole(position, mine_late, other_late)], axis=1)

    def against(coeffs, old):
        size = coeffs.shape[0]
        rows = [sums[:, a:a + size] for a in range(old.shape[0], (DEGREE + 2) * PROBES, PROBES)]
        return jnp.concatenate([old, dot_f32(jnp.concatenate(rows, axis=0), coeffs)], axis=0)

    direction, residual = direction[...], residual[...]
    res_against = against(residual, res_against[...])
    dir_against = against(direction, dir_against[...])
    direction, dir_against = nodes.beta(direction, dir_against, image[...], inverse[...], residual, res_against)
    result = nodes.alpha(direction, None, dir_against, res_against, solution[...])
    share = moments.shape[0]
    coeffs = moment_coeffs(nodes, weights, node[0] * share, share, result)
    onto = dot_f32(sums[:, :PROBES * (DEGREE + 1)], coeffs) * (1.0 / ORDER_DIM)
    for k in range(share):
        projected[k] = onto[:, k * PROBES:(k + 1) * PROBES]
    turned = coeffs.T
    for load in loads:
        load.wait()
    moments[...] = dot_f32(turned, basis[...].reshape((DEGREE + 1) * PROBES, ROWS)).reshape(share, PROBES, ROWS)


def add_body(left, right, out):
    out[...] = left[...] + right[...]


def exchange(value, partner):
    count = lax.axis_size("row")
    return lax.ppermute(value, "row", [(source, partner(source) % count) for source in range(count)])


def core_partner(i):
    return i ^ 1


def chip_partner(i):
    return i + 1 if i % 2 else i - 1


def ring_partner(stage, i):
    y, z, core = i // 16, i // 2 % 8, i % 2
    if stage < 3:
        z = (z ^ 1, z ^ 2, (6, 7, 4, 5, 2, 3, 0, 1)[z])[stage]
    else:
        y = (y ^ 1, y ^ 3)[stage - 3]
    return y * 16 + z * 2 + core


def add(left, right):
    return call(add_body, jax.ShapeDtypeStruct(left.shape, f32), [VMEM] * 2, vmem=4)(left, right)


def stage(value, number):
    return add(value, exchange(value, functools.partial(ring_partner, number)))


def moment_weights():
    orders = np.arange(MOMENTS)[:, None] + 1.0
    angles = np.pi * (np.arange(NODES)[None, :] + 0.5) / NODES
    imag = np.sin(orders * angles) * np.sin(angles) / 8.0
    real = np.cos(orders * angles) / 8.0
    return np.stack([imag, real]).astype(np.float32)


def shards(probes, diag_blocks, couplings, neighbours):
    moment_share = MOMENTS // lax.axis_size("node")
    position = lax.axis_index("row")
    flag = position.reshape(1)
    node = lax.axis_index("node").reshape(1)
    near_by = neighbours.T
    def array(*shape, kind=f32):
        return jax.ShapeDtypeStruct(shape, kind)

    message = array(PROBES, HALF)
    vector = array(PROBES, ROWS)
    pair = array(PROBES, 2 * PROBES)
    double = array(2 * PROBES, HALF)
    band = (array(len(TILES), TILE, TILE, kind=bf16),) * 2
    cross = (array(3, TILE, TILE, kind=bf16),) * 2
    stack = array(DEGREE + 1, PROBES, ROWS)
    copies = pltpu.SemaphoreType.DMA((2,))
    pay_core, pay_chip = call(
        cross_body,
        (message, message),
        [SMEM, SMEM, HBM, HBM],
        vmem=56,
        scratch=[
            pltpu.VMEM((4, 3, BLOCK, BLOCK), f32),
            pltpu.VMEM((PROBES, ROWS), f32),
            pltpu.VMEM((3, TILE, TILE), bf16),
            pltpu.VMEM((3, TILE, TILE), bf16),
            pltpu.SemaphoreType.DMA((5,)),
        ],
    )(near_by, flag, couplings, probes)
    got_core = exchange(pay_core, core_partner)
    got_chip = exchange(pay_chip, chip_partner)
    thi, tlo, uhi, ulo, edge, local, gram = call(
        first_body,
        band + cross + (array(len(EDGE), BLOCK, BLOCK), vector, pair),
        [SMEM, SMEM, VMEM, VMEM, VMEM, HBM],
        flops=10**9,
        bytes_accessed=4 << 20,
        vmem=16,
    )(near_by, flag, diag_blocks, couplings, probes, pay_chip)
    edge, got_chip = lax.optimization_barrier((edge, got_chip))
    edge = exchange(edge, lambda i: i + 1)
    blocks = (thi, tlo, uhi, ulo)
    sent = (vector, message, double, double)
    kept, value, local, spill, pay_core, pay_chip = call(
        start_body,
        (stack, vector) + sent,
        [SMEM] + [VMEM] * 7,
        flops=10**9,
        bytes_accessed=4 << 20,
        out_specs=(HBM,) + (VMEM,) * 5,
        scratch=[copies],
    )(flag, local, got_core, got_chip, *blocks)
    fresh = [probes, value]
    previous = (edge, edge)
    for degree in range(1, DEGREE, 2):
        got_core = exchange(pay_core, core_partner)
        got_chip = exchange(pay_chip, chip_partner)
        more = degree + 2 < DEGREE
        first = degree == 1
        lanes = gram.shape[1] + 2 * PROBES * (len(fresh) - 1)
        sums = (array(PROBES, lanes),) if more else (array(PROBES // 2, lanes),) * 2
        correction, *made = call(
            functools.partial(shadow_body, count=len(fresh), first=first, last=not more),
            (message,) + sums + (cross if first else ()),
            [SMEM] + [VMEM] * (len(fresh) + 3),
            flops=10**9,
            bytes_accessed=2 << 20,
        )(flag, *fresh, gram, *previous)
        if first:
            previous = made[1:]
        if more:
            gram = made[0]
        else:
            early = stage(add(made[0], exchange(made[1], core_partner)), 0)
            early, got_core, got_chip = lax.optimization_barrier((early, got_core, got_chip))
            arrived = exchange(early, functools.partial(ring_partner, 3))
        outs = (stack, vector, vector) + (sent if more else (array(PROBES // 2, 4 * PROBES),) * 2)
        kept, value, after, *rest = call(
            functools.partial(double_body, degree=degree),
            outs,
            [HBM, SMEM] + [VMEM] * 10,
            flops=10**9,
            bytes_accessed=4 << 20,
            out_specs=(HBM,) + (VMEM,) * (len(outs) - 1),
            scratch=[copies],
            aliases=((0, 0),),
        )(kept, flag, fresh[-1], local, spill, correction, got_core, got_chip, *blocks)
        fresh = [fresh[-1], value, after]
        if more:
            local, spill, pay_core, pay_chip = rest
    late, other, arrived = lax.optimization_barrier((*rest, arrived))
    early = add(early, arrived)

    def coeffs(blocks):
        return array(blocks * PROBES, WIDTH)

    work = dict(flops=3 * 10**9, bytes_accessed=4 << 20, vmem=16)
    early, late = lax.optimization_barrier((stage(early, 1), add(late, exchange(other, core_partner))))
    early, late = lax.optimization_barrier((stage(early, 2), stage(late, 3)))
    early, late = lax.optimization_barrier((stage(early, 4), stage(late, 0)))

    def beside(number, body, blocks, specs, *args):
        got = exchange(late, functools.partial(ring_partner, number))
        made = call(body, tuple(map(coeffs, blocks)), specs, **work)(*args)
        got, made = lax.optimization_barrier((got, made))
        return add(late, got), made

    early = (early, exchange(early, core_partner))
    late, state = beside(4, zeroth_body, (3, 3, 9, 9, 1), [SMEM, VMEM, VMEM], flag, *early)
    late, state = beside(2, iterate_body, (5, 5, 7, 7, 3), [VMEM] * 5, *state)
    direction, _, dir_against, _, _ = state
    late, state = beside(1, alpha_body, (7, 1, 7, 5, 5), [VMEM] * 5, *state)
    late = (late, exchange(late, core_partner))
    moments, projected = call(
        moments_body,
        (array(moment_share, PROBES, ROWS), array(moment_share, PROBES, PROBES)),
        [SMEM] * 3 + [VMEM] * 11 + [HBM] * 2,
        vmem=24,
        scratch=[pltpu.VMEM((DEGREE + 1, PROBES, ROWS), f32), pltpu.SemaphoreType.DMA((DEGREE + 1,))],
    )(node, flag, jnp.asarray(moment_weights()), *early, *late, direction, dir_against, *state, probes, kept)
    return (moments, projected)


def solution(mesh):
    placed = (P(None, "row"), P("row", None, None), P("row", None, None, None), P("row", None))
    return jax.shard_map(
        shards,
        mesh=mesh,
        in_specs=placed,
        out_specs=(P("node", None, "row"), P("node", None, None)),
        check_vma=False,
    )
```

```python
import functools
import math

import jax
import jax.numpy as jnp
import numpy as np
from jax import lax
from jax.experimental import pallas as pl
from jax.experimental.pallas import tpu as pltpu
from jax.sharding import PartitionSpec as P

NODES = 8
MOMENTS = 16
REACH = 4
ITERS = 4
PROBES = 32
BLOCK = 128
ROWS = 1024
HALF = 512
TILE = 256
DEGREE = 2 * ITERS - 1
BLOCKS = 512
ORDER_DIM = BLOCKS * BLOCK
SCALE = 16.0

f32 = jnp.float32
bf16 = jnp.bfloat16
highest = lax.Precision.HIGHEST

TILES = [(row, col) for row in range(4) for col in range(row, min(row + 3, 4))]
EDGE = [(row, col) for row in range(REACH) for col in range(row + 1)]

VMEM = pl.BlockSpec(memory_space=pltpu.VMEM)
SMEM = pl.BlockSpec(memory_space=pltpu.SMEM)


HBM = pl.BlockSpec(memory_space=pltpu.HBM)


def call(body, outs, in_specs, flops=0, bytes_accessed=0, vmem=8, scratch=(), out_specs=None, aliases=()):
    return pl.pallas_call(
        body,
        out_shape=outs,
        in_specs=in_specs,
        out_specs=jax.tree.map(lambda _: VMEM, outs) if out_specs is None else out_specs,
        input_output_aliases=dict(aliases),
        scratch_shapes=scratch,
        compiler_params=pltpu.CompilerParams(vmem_limit_bytes=vmem << 20),
        cost_estimate=pl.CostEstimate(flops=flops, bytes_accessed=bytes_accessed, transcendentals=0),
    )


def halves(value):
    high = value.astype(bf16)
    return high, (value - high.astype(f32)).astype(bf16)


def stacked(value):
    high, low = halves(value)
    return jnp.concatenate([high, low], axis=0)


def dot_nn(left, right):
    return lax.dot_general(left, right, (((1,), (0,)), ((), ())), preferred_element_type=f32)


def dot_nt(left, right):
    return lax.dot_general(left, right, (((1,), (1,)), ((), ())), preferred_element_type=f32)


def fold(double):
    half = double.shape[0] // 2
    return double[:half] + double[half:]


def product(dot, pair, high, low):
    return fold(dot(pair, high)) + dot(pair[:pair.shape[0] // 2], low)


def payloads(parity, near, spill, pay_core, pay_chip):
    even = parity == 0
    pay_core[...] = jnp.where(even, spill, near)
    pay_chip[...] = jnp.where(even, near, spill)


def cross_out(tail, uhi, ulo):
    pair = stacked(tail)
    left, right = pair[:, :TILE], pair[:, TILE:]
    first = product(dot_nn, left, uhi[0], ulo[0]) + product(dot_nn, right, uhi[1], ulo[1])
    return jnp.concatenate([first, product(dot_nn, right, uhi[2], ulo[2])], axis=1)


def cross_in(ahead, uhi, ulo):
    pair = stacked(ahead)
    left, right = pair[:, :TILE], pair[:, TILE:]
    second = product(dot_nt, left, uhi[1], ulo[1]) + product(dot_nt, right, uhi[2], ulo[2])
    return jnp.concatenate([product(dot_nt, left, uhi[0], ulo[0]), second], axis=1)


def band_block(step, row, neighbours, position, diag, coup):
    if step == 0:
        return diag * (0.5 / SCALE)
    block = jnp.zeros((BLOCK, BLOCK), f32)
    for f in range(neighbours.shape[0]):
        distance = (neighbours[f, row] - (position * 8 + row)) & (BLOCKS - 1)
        block = block + jnp.where(distance == step, coup[f], 0.0)
    return block * (1.0 / SCALE)


def cross_place(row, col):
    return row // 2 + col // 2, pl.ds(row % 2 * BLOCK, BLOCK), pl.ds(col % 2 * BLOCK, BLOCK)


def cross_zero(uhi, ulo):
    zero = jnp.zeros((BLOCK, BLOCK), bf16)
    for row, col in ((0, 1), (2, 3)):
        uhi[cross_place(row, col)] = zero
        ulo[cross_place(row, col)] = zero


def cross_rows(i, neighbours, position, coup, uhi, ulo, edge=None):
    row = i - 4
    for col in range(row + 1):
        block = band_block(8 + col - i, i, neighbours, position, None, coup)
        uhi[cross_place(row, col)], ulo[cross_place(row, col)] = halves(block)
        if edge is not None:
            edge[EDGE.index((row, col))] = block


def cross_body(neighbours, position, coup_hbm, x_hbm, pay_core, pay_chip, coup, x, uhi, ulo, sems):
    copies = [pltpu.make_async_copy(coup_hbm.at[i], coup.at[i - 4], sems.at[i - 4]) for i in (7, 6, 5, 4)]
    for copy in copies:
        copy.start()
    load = pltpu.make_async_copy(x_hbm, x, sems.at[4])
    load.start()
    cross_zero(uhi, ulo)
    for i, copy in zip((7, 6, 5, 4), copies):
        copy.wait()
        cross_rows(i, neighbours, position[0], coup.at[i - 4], uhi, ulo)
    load.wait()
    payloads(position[0] & 1, x[:, :HALF], cross_out(x[:, HALF:], uhi, ulo), pay_core, pay_chip)


def gram_of(x, before):
    both = jnp.concatenate([before, x], axis=0)
    return lax.dot_general(x, both, (((1,), (1,)), ((), ())), precision=highest, preferred_element_type=f32)


def first_body(neighbours, position, diag, coup, x, after, thi, tlo, uhi, ulo, edge, local, gram):
    zero = jnp.zeros((BLOCK, BLOCK), bf16)
    for tile, (row, col) in enumerate(TILES):
        for up in range(2):
            for across in range(2):
                i, step = 2 * row + up, 2 * (col - row) + across - up
                at = tile, pl.ds(up * BLOCK, BLOCK), pl.ds(across * BLOCK, BLOCK)
                if 0 <= step <= REACH:
                    block = band_block(step, i, neighbours, position[0], diag[i] if step == 0 else None, coup.at[i])
                    thi[at], tlo[at] = halves(block)
                else:
                    thi[at] = zero
                    tlo[at] = zero
    cross_zero(uhi, ulo)
    for i in range(4, 8):
        cross_rows(i, neighbours, position[0], coup.at[i], uhi, ulo, edge)
    value = x[...]
    local[...] = times_local(value, thi, tlo)
    gram[...] = gram_of(value, value)


def times_local(value, thi, tlo):
    pair = stacked(value)
    wide = [jnp.zeros((2 * PROBES, TILE), f32) for _ in range(4)]
    thin = [jnp.zeros((PROBES, TILE), f32) for _ in range(4)]
    for tile, (row, col) in enumerate(TILES):
        high, low = thi[tile], tlo[tile]
        from_row, from_col = pair[:, row * TILE:(row + 1) * TILE], pair[:, col * TILE:(col + 1) * TILE]
        wide[col] = wide[col] + dot_nn(from_row, high)
        thin[col] = thin[col] + dot_nn(from_row[:PROBES], low)
        wide[row] = wide[row] + dot_nt(from_col, high)
        thin[row] = thin[row] + dot_nt(from_col[:PROBES], low)
    return jnp.concatenate([fold(w) + t for w, t in zip(wide, thin)], axis=1)


def joined(local, arrived, inward):
    return jnp.concatenate([local[:, :HALF] + arrived, local[:, HALF:] + inward], axis=1)


def send_two(position, value, thi, tlo, uhi, ulo, local, spill, pay_core, pay_chip):
    following = times_local(value, thi, tlo)
    local[...] = following
    both = cross_out(jnp.concatenate([value[:, HALF:], following[:, HALF:]], axis=0), uhi, ulo)
    spill[...] = both[:PROBES]
    near = jnp.concatenate([value[:, :HALF], following[:, :HALF]], axis=0)
    payloads(position[0] & 1, near, both, pay_core, pay_chip)


def received(position, got_core, got_chip):
    even = position[0] & 1 == 0
    core, chip = got_core[...], got_chip[...]
    return jnp.where(even, core, chip), jnp.where(even, chip, core)


def start_body(position, local, got_core, got_chip, thi, tlo, uhi, ulo, kept, out, *rest):
    *sent, sems = rest
    ahead, arrived = received(position, got_core, got_chip)
    value = joined(local, arrived, cross_in(ahead, uhi, ulo))
    out[...] = value
    keep = pltpu.make_async_copy(out, kept.at[1], sems.at[0])
    keep.start()
    send_two(position, value, thi, tlo, uhi, ulo, *sent)
    keep.wait()


def double_body(
    kept_in, position, before, local, spill, correction, got_core, got_chip, thi, tlo, uhi, ulo, kept, first, second, *rest,
    degree
):
    *sent, sems = rest
    ahead, arrived = received(position, got_core, got_chip)
    ahead = jnp.concatenate([ahead[:PROBES], ahead[PROBES:] + spill[...]], axis=0)
    inward = cross_in(ahead, uhi, ulo)
    value = joined(local, arrived[:PROBES], inward[:PROBES])
    first[...] = value
    keeps = [pltpu.make_async_copy(ref, kept.at[degree + 1 + n], sems.at[n]) for n, ref in enumerate((first, second))]
    keeps[0].start()
    local = times_local(value, thi, tlo)
    after = joined(local, arrived[PROBES:] + correction[...], inward[PROBES:])
    second[...] = after
    keeps[1].start()
    if len(sent) > 2:
        send_two(position, after, thi, tlo, uhi, ulo, *sent)
    else:
        sums = jnp.concatenate([gram_of(value, before[...]), gram_of(after, value)], axis=1)
        store_halves(position, sums, *sent)
    for keep in keeps:
        keep.wait()


def store_halves(position, sums, mine, other):
    upper, lower = sums[:PROBES // 2], sums[PROBES // 2:]
    even = position[0] & 1 == 0
    mine[...] = jnp.where(even, upper, lower)
    other[...] = jnp.where(even, lower, upper)


def shadow_body(position, *refs, count, first, last):
    vectors, (done, up_hi, up_lo), outs = refs[:count], refs[count:count + 3], refs[count + 3:]
    correction, outs = outs[0], outs[1:]
    if first:
        phi, plo = outs[1:]
        cross_zero(phi, plo)
        for n, (row, col) in enumerate(EDGE):
            phi[cross_place(row, col)], plo[cross_place(row, col)] = halves(up_hi[n])
    else:
        phi, plo = up_hi, up_lo
    sums = [done[...]] + [gram_of(vectors[n][...], vectors[n - 1][...]) for n in range(1, count)]
    sums = jnp.concatenate(sums, axis=1)
    if last:
        store_halves(position, sums, *outs)
    else:
        outs[0][...] = sums
    correction[...] = cross_out(cross_in(vectors[-1][:, :HALF], phi, plo), phi, plo)


def dot_f32(left, right):
    return lax.dot_general(left, right, (((1,), (0,)), ((), ())), precision=highest, preferred_element_type=f32)


WIDTH = NODES * PROBES
PANEL = 8


def invert(matrix):
    rows = lax.broadcasted_iota(jnp.int32, (PROBES, WIDTH), 0)
    lanes = lax.broadcasted_iota(jnp.int32, (PROBES, WIDTH), 1) % PROBES
    group = lax.broadcasted_iota(jnp.int32, (PROBES, BLOCK), 1) // PROBES * PROBES
    for start in range(0, PROBES, PANEL):
        columns = [
            jnp.concatenate(
                [jnp.take_along_axis(matrix[:, h:h + BLOCK], group + k, axis=1) for h in range(0, WIDTH, BLOCK)], axis=1
            )
            for k in range(start, start + PANEL)
        ]
        for m in range(PANEL):
            k = start + m
            on_row, on_lane = rows == k, lanes == k
            inverse = 1.0 / columns[m][k:k + 1]
            factor = jnp.where(on_row, -1.0, columns[m])
            scaled = jnp.where(on_lane[:1], 1.0, matrix[k:k + 1]) * inverse
            matrix = jnp.where(on_lane | on_row, 0.0, matrix) - factor * scaled
            for q in range(m + 1, PANEL):
                columns[q] = jnp.where(on_row, 0.0, columns[q]) - factor * (columns[q][k:k + 1] * inverse)
    return matrix


def node_diagonal():
    return (
        lax.broadcasted_iota(jnp.int32, (WIDTH, WIDTH), 0) // PROBES
        == lax.broadcasted_iota(jnp.int32, (WIDTH, WIDTH), 1) // PROBES
    )


def node_shifts():
    node = lax.broadcasted_iota(jnp.int32, (1, WIDTH), 1) // PROBES
    cosine = jnp.zeros((1, WIDTH), f32)
    square = jnp.zeros((1, WIDTH), f32)
    for j in range(NODES):
        angle = math.pi * (j + 0.5) / NODES
        cosine = jnp.where(node == j, np.float32(math.cos(angle)), cosine)
        square = jnp.where(node == j, np.float32(math.sin(angle) ** 2), square)
    return cosine, square


def grown(coeffs, blocks=1):
    return jnp.concatenate([coeffs, jnp.zeros((blocks * PROBES, WIDTH), f32)], axis=0)


def sunk(coeffs, cosine):
    below = jnp.concatenate([jnp.zeros((PROBES, WIDTH), f32), coeffs], axis=0)
    return SCALE * below - cosine * grown(coeffs)


def raised(against, cosine):
    return SCALE * against[PROBES:] - cosine * against[:-PROBES]


class Nodes:
    def __init__(self):
        self.diagonal = node_diagonal()
        self.cosine, self.square = node_shifts()

    def blocks(self, full):
        masked = jnp.where(self.diagonal, full, 0.0)
        return sum(masked[j * PROBES:(j + 1) * PROBES] for j in range(NODES))

    def spread(self, matrix):
        return jnp.where(self.diagonal, jnp.concatenate([matrix] * NODES, axis=0), 0.0)

    def inner(self, left, against):
        return self.blocks(dot_f32(left.T, against[:left.shape[0]]))

    def image(self, direction, dir_against):
        once, once_against = sunk(direction, self.cosine), raised(dir_against, self.cosine)
        image = sunk(once, self.cosine) + self.square * grown(direction, 2)
        image_against = raised(once_against, self.cosine) + self.square * dir_against[:-2 * PROBES]
        return image, image_against

    def alpha(self, direction, residual, dir_against, res_against, solution):
        size = direction.shape[0]
        image, image_against = self.image(direction, dir_against)
        if size == PROBES:
            curvature, now = image_against[:size], res_against[:size]
        else:
            turned = direction.T
            curvature = self.blocks(dot_f32(turned, image_against[:size]))
            now = self.blocks(dot_f32(turned, res_against[:size]))
        inverse = invert(curvature)
        alpha = self.spread(dot_f32(inverse, self.spread(now)))
        if residual is None:
            return grown(solution, 2) + dot_f32(direction, alpha)
        moved = dot_f32(jnp.concatenate([direction, image, image_against], axis=0), alpha)
        part = size + image.shape[0]
        solution = moved[:size] if solution is None else grown(solution, 2) + moved[:size]
        residual = grown(residual, 2) - moved[size:part]
        res_against = res_against[:-2 * PROBES] - moved[part:]
        return image, inverse, residual, res_against, solution

    def beta(self, direction, dir_against, image, inverse, residual, res_against):
        size, count = direction.shape[0], res_against.shape[0]
        beta = self.spread(dot_f32(inverse, self.spread(self.inner(image, res_against))))
        moved = dot_f32(jnp.concatenate([direction, dir_against[:count]], axis=0), beta)
        return residual - grown(moved[:size], 2), res_against - moved[size:]


def moment_coeffs(nodes, weights, first, share, solution):
    applied = sunk(solution, nodes.cosine)
    row = lax.broadcasted_iota(jnp.int32, (PROBES, share * PROBES), 0)
    lane = lax.broadcasted_iota(jnp.int32, (PROBES, share * PROBES), 1)
    imag, real = [], []
    for j in range(NODES):
        for part, (table, sign) in ((imag, (0, 1.0)), (real, (1, -1.0))):
            block = jnp.zeros((PROBES, share * PROBES), f32)
            for k in range(share):
                block = jnp.where(lane == row + k * PROBES, sign * weights[table, first + k, j], block)
            part.append(block)
    left = jnp.concatenate([grown(solution), applied], axis=1)
    return dot_f32(left, jnp.concatenate(imag + real, axis=0))


def whole(position, mine, other):
    even = position[0] & 1 == 0
    upper, lower = jnp.where(even, mine[...], other[...]), jnp.where(even, other[...], mine[...])
    return jnp.concatenate([upper, lower], axis=0)


def store(outs, values):
    for out, value in zip(outs, values):
        out[...] = value


def zeroth_body(position, mine, other, *outs):
    nodes = Nodes()
    sums = whole(position, mine, other)
    against = jnp.concatenate(
        [
            jnp.concatenate([sums[:, at:at + PROBES]] * NODES, axis=1)
            for at in range(PROBES, sums.shape[1], PROBES)
        ],
        axis=0,
    )
    eye = (
        lax.broadcasted_iota(jnp.int32, (PROBES, WIDTH), 0)
        == lax.broadcasted_iota(jnp.int32, (PROBES, WIDTH), 1) % PROBES
    ).astype(f32)
    image, inverse, residual, res_against, solution = nodes.alpha(eye, eye, against, against, None)
    direction, dir_against = nodes.beta(eye, against, image, inverse, residual, res_against)
    store(outs, (direction, residual, dir_against, res_against, solution))


def iterate_body(*refs):
    nodes = Nodes()
    direction, residual, dir_against, res_against, solution = (ref[...] for ref in refs[:5])
    image, inverse, residual, res_against, solution = nodes.alpha(
        direction, residual, dir_against, res_against, solution
    )
    direction, dir_against = nodes.beta(direction, dir_against, image, inverse, residual, res_against)
    store(refs[5:], (direction, residual, dir_against, res_against, solution))


def alpha_body(*refs):
    store(refs[5:], Nodes().alpha(*(ref[...] for ref in refs[:5])))


def moments_body(
    node, position, weights, mine, other, mine_late, other_late, direction, dir_against,
    image, inverse, residual, res_against, solution, k0, kept, moments, projected, basis, sems
):
    loads = [pltpu.make_async_copy(k0, basis.at[0], sems.at[0])]
    loads += [pltpu.make_async_copy(kept.at[d], basis.at[d], sems.at[d]) for d in range(1, DEGREE + 1)]
    for load in loads:
        load.start()
    nodes = Nodes()
    sums = jnp.concatenate([whole(position, mine, other)[:, PROBES:], whole(position, mine_late, other_late)], axis=1)

    def against(coeffs, old):
        size = coeffs.shape[0]
        rows = [sums[:, a:a + size] for a in range(old.shape[0], (DEGREE + 2) * PROBES, PROBES)]
        return jnp.concatenate([old, dot_f32(jnp.concatenate(rows, axis=0), coeffs)], axis=0)

    direction, residual = direction[...], residual[...]
    res_against = against(residual, res_against[...])
    dir_against = against(direction, dir_against[...])
    direction, dir_against = nodes.beta(direction, dir_against, image[...], inverse[...], residual, res_against)
    result = nodes.alpha(direction, None, dir_against, res_against, solution[...])
    share = moments.shape[0]
    coeffs = moment_coeffs(nodes, weights, node[0] * share, share, result)
    onto = dot_f32(sums[:, :PROBES * (DEGREE + 1)], coeffs) * (1.0 / ORDER_DIM)
    for k in range(share):
        projected[k] = onto[:, k * PROBES:(k + 1) * PROBES]
    turned = coeffs.T
    for load in loads:
        load.wait()
    moments[...] = dot_f32(turned, basis[...].reshape((DEGREE + 1) * PROBES, ROWS)).reshape(share, PROBES, ROWS)


def add_body(left, right, out):
    out[...] = left[...] + right[...]


def pack_body(early, early_got, late, late_got, out):
    lanes = early.shape[1]
    out[:, :lanes] = early[...] + early_got[...]
    out[:, lanes:] = late[...] + late_got[...]


def exchange(value, partner):
    count = lax.axis_size("row")
    return lax.ppermute(value, "row", [(source, partner(source) % count) for source in range(count)])


def core_partner(i):
    return i ^ 1


def chip_partner(i):
    return i + 1 if i % 2 else i - 1


def ring_partner(stage, i):
    y, z, core = i // 16, i // 2 % 8, i % 2
    if stage < 3:
        z = (z ^ 1, z ^ 2, (6, 7, 4, 5, 2, 3, 0, 1)[z])[stage]
    else:
        y = (y ^ 1, y ^ 3)[stage - 3]
    return y * 16 + z * 2 + core


def add(left, right):
    return call(add_body, jax.ShapeDtypeStruct(left.shape, f32), [VMEM] * 2, vmem=4)(left, right)


def stage(value, number):
    return add(value, exchange(value, functools.partial(ring_partner, number)))


def moment_weights():
    orders = np.arange(MOMENTS)[:, None] + 1.0
    angles = np.pi * (np.arange(NODES)[None, :] + 0.5) / NODES
    imag = np.sin(orders * angles) * np.sin(angles) / 8.0
    real = np.cos(orders * angles) / 8.0
    return np.stack([imag, real]).astype(np.float32)


def shards(probes, diag_blocks, couplings, neighbours):
    moment_share = MOMENTS // lax.axis_size("node")
    position = lax.axis_index("row")
    flag = position.reshape(1)
    node = lax.axis_index("node").reshape(1)
    near_by = neighbours.T
    def array(*shape, kind=f32):
        return jax.ShapeDtypeStruct(shape, kind)

    message = array(PROBES, HALF)
    vector = array(PROBES, ROWS)
    pair = array(PROBES, 2 * PROBES)
    double = array(2 * PROBES, HALF)
    band = (array(len(TILES), TILE, TILE, kind=bf16),) * 2
    cross = (array(3, TILE, TILE, kind=bf16),) * 2
    stack = array(DEGREE + 1, PROBES, ROWS)
    copies = pltpu.SemaphoreType.DMA((2,))
    pay_core, pay_chip = call(
        cross_body,
        (message, message),
        [SMEM, SMEM, HBM, HBM],
        vmem=56,
        scratch=[
            pltpu.VMEM((4, 3, BLOCK, BLOCK), f32),
            pltpu.VMEM((PROBES, ROWS), f32),
            pltpu.VMEM((3, TILE, TILE), bf16),
            pltpu.VMEM((3, TILE, TILE), bf16),
            pltpu.SemaphoreType.DMA((5,)),
        ],
    )(near_by, flag, couplings, probes)
    got_core = exchange(pay_core, core_partner)
    got_chip = exchange(pay_chip, chip_partner)
    thi, tlo, uhi, ulo, edge, local, gram = call(
        first_body,
        band + cross + (array(len(EDGE), BLOCK, BLOCK), vector, pair),
        [SMEM, SMEM, VMEM, VMEM, VMEM, HBM],
        flops=10**9,
        bytes_accessed=4 << 20,
        vmem=16,
    )(near_by, flag, diag_blocks, couplings, probes, got_core)
    edge, got_chip = lax.optimization_barrier((edge, got_chip))
    edge = exchange(edge, lambda i: i + 1)
    blocks = (thi, tlo, uhi, ulo)
    sent = (vector, message, double, double)
    kept, value, local, spill, pay_core, pay_chip = call(
        start_body,
        (stack, vector) + sent,
        [SMEM] + [VMEM] * 7,
        flops=10**9,
        bytes_accessed=4 << 20,
        out_specs=(HBM,) + (VMEM,) * 5,
        scratch=[copies],
    )(flag, local, got_core, got_chip, *blocks)
    fresh = [probes, value]
    previous = (edge, edge)
    for degree in range(1, DEGREE, 2):
        got_core = exchange(pay_core, core_partner)
        got_chip = exchange(pay_chip, chip_partner)
        more = degree + 2 < DEGREE
        first = degree == 1
        lanes = gram.shape[1] + 2 * PROBES * (len(fresh) - 1)
        sums = (array(PROBES, lanes),) if more else (array(PROBES // 2, lanes),) * 2
        correction, *made = call(
            functools.partial(shadow_body, count=len(fresh), first=first, last=not more),
            (message,) + sums + (cross if first else ()),
            [SMEM] + [VMEM] * (len(fresh) + 3),
            flops=10**9,
            bytes_accessed=2 << 20,
        )(flag, *fresh, gram, *previous)
        if first:
            previous = made[1:]
        if more:
            gram = made[0]
        else:
            early = stage(add(made[0], exchange(made[1], core_partner)), 0)
            early, got_core, got_chip = lax.optimization_barrier((early, got_core, got_chip))
            arrived = exchange(early, functools.partial(ring_partner, 3))
        outs = (stack, vector, vector) + (sent if more else (array(PROBES // 2, 4 * PROBES),) * 2)
        kept, value, after, *rest = call(
            functools.partial(double_body, degree=degree),
            outs,
            [HBM, SMEM] + [VMEM] * 10,
            flops=10**9,
            bytes_accessed=4 << 20,
            out_specs=(HBM,) + (VMEM,) * (len(outs) - 1),
            scratch=[copies],
            aliases=((0, 0),),
        )(kept, flag, fresh[-1], local, spill, correction, got_core, got_chip, *blocks)
        fresh = [fresh[-1], value, after]
        if more:
            local, spill, pay_core, pay_chip = rest
    late, other, arrived = lax.optimization_barrier((*rest, arrived))
    early = add(early, arrived)

    def coeffs(blocks):
        return array(blocks * PROBES, WIDTH)

    work = dict(flops=3 * 10**9, bytes_accessed=4 << 20, vmem=16)
    lanes = early.shape[1]
    pack = call(pack_body, array(PROBES // 2, lanes + late.shape[1]), [VMEM] * 4, vmem=4)(
        early, exchange(early, functools.partial(ring_partner, 1)), late, exchange(other, core_partner)
    )
    pack = stage(stage(pack, 2), 4)
    early, late = pack[:, :lanes], pack[:, lanes:]

    def beside(number, body, blocks, specs, *args):
        got = exchange(late, functools.partial(ring_partner, number))
        made = call(body, tuple(map(coeffs, blocks)), specs, **work)(*args)
        got, made = lax.optimization_barrier((got, made))
        return add(late, got), made

    early = (early, exchange(early, core_partner))
    late, state = beside(3, zeroth_body, (3, 3, 9, 9, 1), [SMEM, VMEM, VMEM], flag, *early)
    late, state = beside(0, iterate_body, (5, 5, 7, 7, 3), [VMEM] * 5, *state)
    direction, _, dir_against, _, _ = state
    late, state = beside(1, alpha_body, (7, 1, 7, 5, 5), [VMEM] * 5, *state)
    late = (late, exchange(late, core_partner))
    moments, projected = call(
        moments_body,
        (array(moment_share, PROBES, ROWS), array(moment_share, PROBES, PROBES)),
        [SMEM] * 3 + [VMEM] * 11 + [HBM] * 2,
        vmem=24,
        scratch=[pltpu.VMEM((DEGREE + 1, PROBES, ROWS), f32), pltpu.SemaphoreType.DMA((DEGREE + 1,))],
    )(node, flag, jnp.asarray(moment_weights()), *early, *late, direction, dir_against, *state, probes, kept)
    return (moments, projected)


def solution(mesh):
    placed = (P(None, "row"), P("row", None, None), P("row", None, None, None), P("row", None))
    return jax.shard_map(
        shards,
        mesh=mesh,
        in_specs=placed,
        out_specs=(P("node", None, "row"), P("node", None, None)),
        check_vma=False,
    )
```

```python
import functools
import math

import jax
import jax.numpy as jnp
import numpy as np
from jax import lax
from jax.experimental import pallas as pl
from jax.experimental.pallas import tpu as pltpu
from jax.sharding import PartitionSpec as P

NODES = 8
MOMENTS = 16
REACH = 4
ITERS = 4
PROBES = 32
BLOCK = 128
ROWS = 1024
HALF = 512
TILE = 256
DEGREE = 2 * ITERS - 1
BLOCKS = 512
ORDER_DIM = BLOCKS * BLOCK
SCALE = 16.0

f32 = jnp.float32
bf16 = jnp.bfloat16
highest = lax.Precision.HIGHEST

TILES = [(row, col) for row in range(4) for col in range(row, min(row + 3, 4))]
EDGE = [(row, col) for row in range(REACH) for col in range(row + 1)]

VMEM = pl.BlockSpec(memory_space=pltpu.VMEM)
SMEM = pl.BlockSpec(memory_space=pltpu.SMEM)


HBM = pl.BlockSpec(memory_space=pltpu.HBM)


def call(body, outs, in_specs, flops=0, bytes_accessed=0, vmem=8, scratch=(), out_specs=None, aliases=()):
    return pl.pallas_call(
        body,
        out_shape=outs,
        in_specs=in_specs,
        out_specs=jax.tree.map(lambda _: VMEM, outs) if out_specs is None else out_specs,
        input_output_aliases=dict(aliases),
        scratch_shapes=scratch,
        compiler_params=pltpu.CompilerParams(vmem_limit_bytes=vmem << 20),
        cost_estimate=pl.CostEstimate(flops=flops, bytes_accessed=bytes_accessed, transcendentals=0),
    )


def halves(value):
    high = value.astype(bf16)
    return high, (value - high.astype(f32)).astype(bf16)


def stacked(value):
    high, low = halves(value)
    return jnp.concatenate([high, low], axis=0)


def dot_nn(left, right):
    return lax.dot_general(left, right, (((1,), (0,)), ((), ())), preferred_element_type=f32)


def dot_nt(left, right):
    return lax.dot_general(left, right, (((1,), (1,)), ((), ())), preferred_element_type=f32)


def fold(double):
    half = double.shape[0] // 2
    return double[:half] + double[half:]


def product(dot, pair, high, low):
    return fold(dot(pair, high)) + dot(pair[:pair.shape[0] // 2], low)


def payloads(parity, near, spill, pay_core, pay_chip):
    even = parity == 0
    pay_core[...] = jnp.where(even, spill, near)
    pay_chip[...] = jnp.where(even, near, spill)


def cross_out(tail, uhi, ulo):
    pair = stacked(tail)
    left, right = pair[:, :TILE], pair[:, TILE:]
    first = product(dot_nn, left, uhi[0], ulo[0]) + product(dot_nn, right, uhi[1], ulo[1])
    return jnp.concatenate([first, product(dot_nn, right, uhi[2], ulo[2])], axis=1)


def cross_in(ahead, uhi, ulo):
    pair = stacked(ahead)
    left, right = pair[:, :TILE], pair[:, TILE:]
    second = product(dot_nt, left, uhi[1], ulo[1]) + product(dot_nt, right, uhi[2], ulo[2])
    return jnp.concatenate([product(dot_nt, left, uhi[0], ulo[0]), second], axis=1)


def band_block(step, row, neighbours, position, diag, coup):
    if step == 0:
        return diag * (0.5 / SCALE)
    block = jnp.zeros((BLOCK, BLOCK), f32)
    for f in range(neighbours.shape[0]):
        distance = (neighbours[f, row] - (position * 8 + row)) & (BLOCKS - 1)
        block = block + jnp.where(distance == step, coup[f], 0.0)
    return block * (1.0 / SCALE)


def cross_place(row, col):
    return row // 2 + col // 2, pl.ds(row % 2 * BLOCK, BLOCK), pl.ds(col % 2 * BLOCK, BLOCK)


def cross_zero(uhi, ulo):
    zero = jnp.zeros((BLOCK, BLOCK), bf16)
    for row, col in ((0, 1), (2, 3)):
        uhi[cross_place(row, col)] = zero
        ulo[cross_place(row, col)] = zero


def cross_rows(i, neighbours, position, coup, uhi, ulo, edge=None):
    row = i - 4
    for col in range(row + 1):
        block = band_block(8 + col - i, i, neighbours, position, None, coup)
        uhi[cross_place(row, col)], ulo[cross_place(row, col)] = halves(block)
        if edge is not None:
            edge[EDGE.index((row, col))] = block


def cross_body(neighbours, position, coup_hbm, x_hbm, pay_core, pay_chip, coup, x, uhi, ulo, sems):
    copies = [pltpu.make_async_copy(coup_hbm.at[i], coup.at[i - 4], sems.at[i - 4]) for i in (7, 6, 5, 4)]
    for copy in copies:
        copy.start()
    load = pltpu.make_async_copy(x_hbm, x, sems.at[4])
    load.start()
    cross_zero(uhi, ulo)
    for i, copy in zip((7, 6, 5, 4), copies):
        copy.wait()
        cross_rows(i, neighbours, position[0], coup.at[i - 4], uhi, ulo)
    load.wait()
    payloads(position[0] & 1, x[:, :HALF], cross_out(x[:, HALF:], uhi, ulo), pay_core, pay_chip)


def gram_of(x, before):
    both = jnp.concatenate([before, x], axis=0)
    return lax.dot_general(x, both, (((1,), (1,)), ((), ())), precision=highest, preferred_element_type=f32)


def first_body(neighbours, position, diag, coup, x, after, thi, tlo, uhi, ulo, edge, local, gram):
    zero = jnp.zeros((BLOCK, BLOCK), bf16)
    for tile, (row, col) in enumerate(TILES):
        for up in range(2):
            for across in range(2):
                i, step = 2 * row + up, 2 * (col - row) + across - up
                at = tile, pl.ds(up * BLOCK, BLOCK), pl.ds(across * BLOCK, BLOCK)
                if 0 <= step <= REACH:
                    block = band_block(step, i, neighbours, position[0], diag[i] if step == 0 else None, coup.at[i])
                    thi[at], tlo[at] = halves(block)
                else:
                    thi[at] = zero
                    tlo[at] = zero
    cross_zero(uhi, ulo)
    for i in range(4, 8):
        cross_rows(i, neighbours, position[0], coup.at[i], uhi, ulo, edge)
    value = x[...]
    local[...] = times_local(value, thi, tlo)
    gram[...] = gram_of(value, value)


def times_local(value, thi, tlo):
    pair = stacked(value)
    wide = [jnp.zeros((2 * PROBES, TILE), f32) for _ in range(4)]
    thin = [jnp.zeros((PROBES, TILE), f32) for _ in range(4)]
    for tile, (row, col) in enumerate(TILES):
        high, low = thi[tile], tlo[tile]
        from_row, from_col = pair[:, row * TILE:(row + 1) * TILE], pair[:, col * TILE:(col + 1) * TILE]
        wide[col] = wide[col] + dot_nn(from_row, high)
        thin[col] = thin[col] + dot_nn(from_row[:PROBES], low)
        wide[row] = wide[row] + dot_nt(from_col, high)
        thin[row] = thin[row] + dot_nt(from_col[:PROBES], low)
    return jnp.concatenate([fold(w) + t for w, t in zip(wide, thin)], axis=1)


def joined(local, arrived, inward):
    return jnp.concatenate([local[:, :HALF] + arrived, local[:, HALF:] + inward], axis=1)


def send_two(position, value, thi, tlo, uhi, ulo, local, spill, pay_core, pay_chip):
    following = times_local(value, thi, tlo)
    local[...] = following
    both = cross_out(jnp.concatenate([value[:, HALF:], following[:, HALF:]], axis=0), uhi, ulo)
    spill[...] = both[:PROBES]
    near = jnp.concatenate([value[:, :HALF], following[:, :HALF]], axis=0)
    payloads(position[0] & 1, near, both, pay_core, pay_chip)


def received(position, got_core, got_chip):
    even = position[0] & 1 == 0
    core, chip = got_core[...], got_chip[...]
    return jnp.where(even, core, chip), jnp.where(even, chip, core)


def start_body(position, local, got_core, got_chip, thi, tlo, uhi, ulo, kept, out, *rest):
    *sent, sems = rest
    ahead, arrived = received(position, got_core, got_chip)
    value = joined(local, arrived, cross_in(ahead, uhi, ulo))
    out[...] = value
    keep = pltpu.make_async_copy(out, kept.at[1], sems.at[0])
    keep.start()
    send_two(position, value, thi, tlo, uhi, ulo, *sent)
    keep.wait()


def double_body(
    kept_in, position, before, local, spill, correction, got_core, got_chip, thi, tlo, uhi, ulo, kept, first, second, *rest,
    degree
):
    *sent, sems = rest
    ahead, arrived = received(position, got_core, got_chip)
    ahead = jnp.concatenate([ahead[:PROBES], ahead[PROBES:] + spill[...]], axis=0)
    inward = cross_in(ahead, uhi, ulo)
    value = joined(local, arrived[:PROBES], inward[:PROBES])
    first[...] = value
    keeps = [pltpu.make_async_copy(ref, kept.at[degree + 1 + n], sems.at[n]) for n, ref in enumerate((first, second))]
    keeps[0].start()
    local = times_local(value, thi, tlo)
    after = joined(local, arrived[PROBES:] + correction[...], inward[PROBES:])
    second[...] = after
    keeps[1].start()
    if len(sent) > 2:
        send_two(position, after, thi, tlo, uhi, ulo, *sent)
    else:
        both = gram_of(jnp.concatenate([value, after], axis=0), before[...])
        sums = jnp.concatenate([both[:PROBES, :2 * PROBES], both[PROBES:, PROBES:]], axis=1)
        store_halves(position, sums, *sent)
    for keep in keeps:
        keep.wait()


def store_halves(position, sums, mine, other):
    upper, lower = sums[:PROBES // 2], sums[PROBES // 2:]
    even = position[0] & 1 == 0
    mine[...] = jnp.where(even, upper, lower)
    other[...] = jnp.where(even, lower, upper)


def shadow_body(position, *refs, count, first, last):
    vectors, (done, up_hi, up_lo), outs = refs[:count], refs[count:count + 3], refs[count + 3:]
    correction, outs = outs[0], outs[1:]
    if first:
        phi, plo = outs[1:]
        cross_zero(phi, plo)
        for n, (row, col) in enumerate(EDGE):
            phi[cross_place(row, col)], plo[cross_place(row, col)] = halves(up_hi[n])
    else:
        phi, plo = up_hi, up_lo
    sums = [done[...]] + [gram_of(vectors[n][...], vectors[n - 1][...]) for n in range(1, count)]
    sums = jnp.concatenate(sums, axis=1)
    if last:
        store_halves(position, sums, *outs)
    else:
        outs[0][...] = sums
    correction[...] = cross_out(cross_in(vectors[-1][:, :HALF], phi, plo), phi, plo)


def dot_f32(left, right):
    return lax.dot_general(left, right, (((1,), (0,)), ((), ())), precision=highest, preferred_element_type=f32)


WIDTH = NODES * PROBES
PANEL = 8


def invert(matrix):
    rows = lax.broadcasted_iota(jnp.int32, (PROBES, WIDTH), 0)
    lanes = lax.broadcasted_iota(jnp.int32, (PROBES, WIDTH), 1) % PROBES
    group = lax.broadcasted_iota(jnp.int32, (PROBES, BLOCK), 1) // PROBES * PROBES
    for start in range(0, PROBES, PANEL):
        columns = [
            jnp.concatenate(
                [jnp.take_along_axis(matrix[:, h:h + BLOCK], group + k, axis=1) for h in range(0, WIDTH, BLOCK)], axis=1
            )
            for k in range(start, start + PANEL)
        ]
        for m in range(PANEL):
            k = start + m
            on_row, on_lane = rows == k, lanes == k
            inverse = 1.0 / columns[m][k:k + 1]
            factor = jnp.where(on_row, -1.0, columns[m])
            scaled = jnp.where(on_lane[:1], 1.0, matrix[k:k + 1]) * inverse
            matrix = jnp.where(on_lane | on_row, 0.0, matrix) - factor * scaled
            for q in range(m + 1, PANEL):
                columns[q] = jnp.where(on_row, 0.0, columns[q]) - factor * (columns[q][k:k + 1] * inverse)
    return matrix


def node_diagonal():
    return (
        lax.broadcasted_iota(jnp.int32, (WIDTH, WIDTH), 0) // PROBES
        == lax.broadcasted_iota(jnp.int32, (WIDTH, WIDTH), 1) // PROBES
    )


def node_shifts():
    node = lax.broadcasted_iota(jnp.int32, (1, WIDTH), 1) // PROBES
    cosine = jnp.zeros((1, WIDTH), f32)
    square = jnp.zeros((1, WIDTH), f32)
    for j in range(NODES):
        angle = math.pi * (j + 0.5) / NODES
        cosine = jnp.where(node == j, np.float32(math.cos(angle)), cosine)
        square = jnp.where(node == j, np.float32(math.sin(angle) ** 2), square)
    return cosine, square


def grown(coeffs, blocks=1):
    return jnp.concatenate([coeffs, jnp.zeros((blocks * PROBES, WIDTH), f32)], axis=0)


def sunk(coeffs, cosine):
    below = jnp.concatenate([jnp.zeros((PROBES, WIDTH), f32), coeffs], axis=0)
    return SCALE * below - cosine * grown(coeffs)


def raised(against, cosine):
    return SCALE * against[PROBES:] - cosine * against[:-PROBES]


class Nodes:
    def __init__(self):
        self.diagonal = node_diagonal()
        self.cosine, self.square = node_shifts()

    def blocks(self, full):
        masked = jnp.where(self.diagonal, full, 0.0)
        return sum(masked[j * PROBES:(j + 1) * PROBES] for j in range(NODES))

    def spread(self, matrix):
        return jnp.where(self.diagonal, jnp.concatenate([matrix] * NODES, axis=0), 0.0)

    def inner(self, left, against):
        return self.blocks(dot_f32(left.T, against[:left.shape[0]]))

    def image(self, direction, dir_against):
        once, once_against = sunk(direction, self.cosine), raised(dir_against, self.cosine)
        image = sunk(once, self.cosine) + self.square * grown(direction, 2)
        image_against = raised(once_against, self.cosine) + self.square * dir_against[:-2 * PROBES]
        return image, image_against

    def alpha(self, direction, residual, dir_against, res_against, solution):
        size = direction.shape[0]
        image, image_against = self.image(direction, dir_against)
        if size == PROBES:
            curvature, now = image_against[:size], res_against[:size]
        else:
            turned = direction.T
            both = dot_f32(turned, jnp.concatenate([image_against[:size], res_against[:size]], axis=1))
            curvature, now = self.blocks(both[:, :WIDTH]), self.blocks(both[:, WIDTH:])
        inverse = invert(curvature)
        alpha = self.spread(dot_f32(inverse, self.spread(now)))
        if residual is None:
            return grown(solution, 2) + dot_f32(direction, alpha)
        moved = dot_f32(jnp.concatenate([direction, image, image_against], axis=0), alpha)
        part = size + image.shape[0]
        solution = moved[:size] if solution is None else grown(solution, 2) + moved[:size]
        residual = grown(residual, 2) - moved[size:part]
        res_against = res_against[:-2 * PROBES] - moved[part:]
        return image, inverse, residual, res_against, solution

    def beta(self, direction, dir_against, image, inverse, residual, res_against):
        size, count = direction.shape[0], res_against.shape[0]
        beta = self.spread(dot_f32(inverse, self.spread(self.inner(image, res_against))))
        moved = dot_f32(jnp.concatenate([direction, dir_against[:count]], axis=0), beta)
        return residual - grown(moved[:size], 2), res_against - moved[size:]


def moment_coeffs(nodes, weights, first, share, solution):
    applied = sunk(solution, nodes.cosine)
    row = lax.broadcasted_iota(jnp.int32, (PROBES, share * PROBES), 0)
    lane = lax.broadcasted_iota(jnp.int32, (PROBES, share * PROBES), 1)
    imag, real = [], []
    for j in range(NODES):
        for part, (table, sign) in ((imag, (0, 1.0)), (real, (1, -1.0))):
            block = jnp.zeros((PROBES, share * PROBES), f32)
            for k in range(share):
                block = jnp.where(lane == row + k * PROBES, sign * weights[table, first + k, j], block)
            part.append(block)
    left = jnp.concatenate([grown(solution), applied], axis=1)
    return dot_f32(left, jnp.concatenate(imag + real, axis=0))


def whole(position, mine, other):
    even = position[0] & 1 == 0
    upper, lower = jnp.where(even, mine[...], other[...]), jnp.where(even, other[...], mine[...])
    return jnp.concatenate([upper, lower], axis=0)


def store(outs, values):
    for out, value in zip(outs, values):
        out[...] = value


def zeroth_body(position, mine, other, *outs):
    nodes = Nodes()
    sums = whole(position, mine, other)
    against = jnp.concatenate(
        [
            jnp.concatenate([sums[:, at:at + PROBES]] * NODES, axis=1)
            for at in range(PROBES, sums.shape[1], PROBES)
        ],
        axis=0,
    )
    eye = (
        lax.broadcasted_iota(jnp.int32, (PROBES, WIDTH), 0)
        == lax.broadcasted_iota(jnp.int32, (PROBES, WIDTH), 1) % PROBES
    ).astype(f32)
    image, inverse, residual, res_against, solution = nodes.alpha(eye, eye, against, against, None)
    direction, dir_against = nodes.beta(eye, against, image, inverse, residual, res_against)
    store(outs, (direction, residual, dir_against, res_against, solution))


def iterate_body(*refs):
    nodes = Nodes()
    direction, residual, dir_against, res_against, solution = (ref[...] for ref in refs[:5])
    image, inverse, residual, res_against, solution = nodes.alpha(
        direction, residual, dir_against, res_against, solution
    )
    direction, dir_against = nodes.beta(direction, dir_against, image, inverse, residual, res_against)
    store(refs[5:], (direction, residual, dir_against, res_against, solution))


def alpha_body(*refs):
    store(refs[5:], Nodes().alpha(*(ref[...] for ref in refs[:5])))


def moments_body(
    node, position, weights, mine, other, mine_late, other_late, direction, dir_against,
    image, inverse, residual, res_against, solution, k0, kept, moments, projected, basis, sems
):
    loads = [pltpu.make_async_copy(k0, basis.at[0], sems.at[0])]
    loads += [pltpu.make_async_copy(kept.at[d], basis.at[d], sems.at[d]) for d in range(1, DEGREE + 1)]
    for load in loads:
        load.start()
    nodes = Nodes()
    sums = jnp.concatenate([whole(position, mine, other)[:, PROBES:], whole(position, mine_late, other_late)], axis=1)

    def against(coeffs, old):
        size = coeffs.shape[0]
        rows = [sums[:, a:a + size] for a in range(old.shape[0], (DEGREE + 2) * PROBES, PROBES)]
        return jnp.concatenate([old, dot_f32(jnp.concatenate(rows, axis=0), coeffs)], axis=0)

    direction, residual = direction[...], residual[...]
    res_against = against(residual, res_against[...])
    dir_against = against(direction, dir_against[...])
    direction, dir_against = nodes.beta(direction, dir_against, image[...], inverse[...], residual, res_against)
    result = nodes.alpha(direction, None, dir_against, res_against, solution[...])
    share = moments.shape[0]
    coeffs = moment_coeffs(nodes, weights, node[0] * share, share, result)
    onto = dot_f32(sums[:, :PROBES * (DEGREE + 1)], coeffs) * (1.0 / ORDER_DIM)
    for k in range(share):
        projected[k] = onto[:, k * PROBES:(k + 1) * PROBES]
    turned = coeffs.T
    for load in loads:
        load.wait()
    moments[...] = dot_f32(turned, basis[...].reshape((DEGREE + 1) * PROBES, ROWS)).reshape(share, PROBES, ROWS)


def add_body(left, right, out):
    out[...] = left[...] + right[...]


def pack_body(early, early_got, late, late_got, out):
    lanes = early.shape[1]
    out[:, :lanes] = early[...] + early_got[...]
    out[:, lanes:] = late[...] + late_got[...]


def exchange(value, partner):
    count = lax.axis_size("row")
    return lax.ppermute(value, "row", [(source, partner(source) % count) for source in range(count)])


def core_partner(i):
    return i ^ 1


def chip_partner(i):
    return i + 1 if i % 2 else i - 1


def ring_partner(stage, i):
    y, z, core = i // 16, i // 2 % 8, i % 2
    if stage < 3:
        z = (z ^ 1, z ^ 2, (6, 7, 4, 5, 2, 3, 0, 1)[z])[stage]
    else:
        y = (y ^ 1, y ^ 3)[stage - 3]
    return y * 16 + z * 2 + core


def add(left, right):
    return call(add_body, jax.ShapeDtypeStruct(left.shape, f32), [VMEM] * 2, vmem=4)(left, right)


def stage(value, number):
    return add(value, exchange(value, functools.partial(ring_partner, number)))


def moment_weights():
    orders = np.arange(MOMENTS)[:, None] + 1.0
    angles = np.pi * (np.arange(NODES)[None, :] + 0.5) / NODES
    imag = np.sin(orders * angles) * np.sin(angles) / 8.0
    real = np.cos(orders * angles) / 8.0
    return np.stack([imag, real]).astype(np.float32)


def shards(probes, diag_blocks, couplings, neighbours):
    moment_share = MOMENTS // lax.axis_size("node")
    position = lax.axis_index("row")
    flag = position.reshape(1)
    node = lax.axis_index("node").reshape(1)
    near_by = neighbours.T
    def array(*shape, kind=f32):
        return jax.ShapeDtypeStruct(shape, kind)

    message = array(PROBES, HALF)
    vector = array(PROBES, ROWS)
    pair = array(PROBES, 2 * PROBES)
    double = array(2 * PROBES, HALF)
    band = (array(len(TILES), TILE, TILE, kind=bf16),) * 2
    cross = (array(3, TILE, TILE, kind=bf16),) * 2
    stack = array(DEGREE + 1, PROBES, ROWS)
    copies = pltpu.SemaphoreType.DMA((2,))
    pay_core, pay_chip = call(
        cross_body,
        (message, message),
        [SMEM, SMEM, HBM, HBM],
        vmem=56,
        scratch=[
            pltpu.VMEM((4, 3, BLOCK, BLOCK), f32),
            pltpu.VMEM((PROBES, ROWS), f32),
            pltpu.VMEM((3, TILE, TILE), bf16),
            pltpu.VMEM((3, TILE, TILE), bf16),
            pltpu.SemaphoreType.DMA((5,)),
        ],
    )(near_by, flag, couplings, probes)
    got_core = exchange(pay_core, core_partner)
    got_chip = exchange(pay_chip, chip_partner)
    thi, tlo, uhi, ulo, edge, local, gram = call(
        first_body,
        band + cross + (array(len(EDGE), BLOCK, BLOCK), vector, pair),
        [SMEM, SMEM, VMEM, VMEM, VMEM, HBM],
        flops=10**9,
        bytes_accessed=4 << 20,
        vmem=16,
    )(near_by, flag, diag_blocks, couplings, probes, got_core)
    edge, got_chip = lax.optimization_barrier((edge, got_chip))
    edge = exchange(edge, lambda i: i + 1)
    blocks = (thi, tlo, uhi, ulo)
    sent = (vector, message, double, double)
    kept, value, local, spill, pay_core, pay_chip = call(
        start_body,
        (stack, vector) + sent,
        [SMEM] + [VMEM] * 7,
        flops=10**9,
        bytes_accessed=4 << 20,
        out_specs=(HBM,) + (VMEM,) * 5,
        scratch=[copies],
    )(flag, local, got_core, got_chip, *blocks)
    fresh = [probes, value]
    previous = (edge, edge)
    for degree in range(1, DEGREE, 2):
        got_core = exchange(pay_core, core_partner)
        got_chip = exchange(pay_chip, chip_partner)
        more = degree + 2 < DEGREE
        first = degree == 1
        lanes = gram.shape[1] + 2 * PROBES * (len(fresh) - 1)
        sums = (array(PROBES, lanes),) if more else (array(PROBES // 2, lanes),) * 2
        correction, *made = call(
            functools.partial(shadow_body, count=len(fresh), first=first, last=not more),
            (message,) + sums + (cross if first else ()),
            [SMEM] + [VMEM] * (len(fresh) + 3),
            flops=10**9,
            bytes_accessed=2 << 20,
        )(flag, *fresh, gram, *previous)
        if first:
            previous = made[1:]
        if more:
            gram = made[0]
        else:
            early = stage(add(made[0], exchange(made[1], core_partner)), 0)
            early, got_core, got_chip = lax.optimization_barrier((early, got_core, got_chip))
            arrived = exchange(early, functools.partial(ring_partner, 3))
        outs = (stack, vector, vector) + (sent if more else (array(PROBES // 2, 4 * PROBES),) * 2)
        kept, value, after, *rest = call(
            functools.partial(double_body, degree=degree),
            outs,
            [HBM, SMEM] + [VMEM] * 10,
            flops=10**9,
            bytes_accessed=4 << 20,
            out_specs=(HBM,) + (VMEM,) * (len(outs) - 1),
            scratch=[copies],
            aliases=((0, 0),),
        )(kept, flag, fresh[-1], local, spill, correction, got_core, got_chip, *blocks)
        fresh = [fresh[-1], value, after]
        if more:
            local, spill, pay_core, pay_chip = rest
    late, other, arrived = lax.optimization_barrier((*rest, arrived))
    early = add(early, arrived)

    def coeffs(blocks):
        return array(blocks * PROBES, WIDTH)

    work = dict(flops=3 * 10**9, bytes_accessed=4 << 20, vmem=16)
    lanes = early.shape[1]
    pack = call(pack_body, array(PROBES // 2, lanes + late.shape[1]), [VMEM] * 4, vmem=4)(
        early, exchange(early, functools.partial(ring_partner, 1)), late, exchange(other, core_partner)
    )
    pack = stage(stage(pack, 2), 4)
    early, late = pack[:, :lanes], pack[:, lanes:]

    def beside(number, body, blocks, specs, *args):
        got = exchange(late, functools.partial(ring_partner, number))
        made = call(body, tuple(map(coeffs, blocks)), specs, **work)(*args)
        got, made = lax.optimization_barrier((got, made))
        return add(late, got), made

    early = (early, exchange(early, core_partner))
    late, state = beside(3, zeroth_body, (3, 3, 9, 9, 1), [SMEM, VMEM, VMEM], flag, *early)
    late, state = beside(0, iterate_body, (5, 5, 7, 7, 3), [VMEM] * 5, *state)
    direction, _, dir_against, _, _ = state
    late, state = beside(1, alpha_body, (7, 1, 7, 5, 5), [VMEM] * 5, *state)
    late = (late, exchange(late, core_partner))
    moments, projected = call(
        moments_body,
        (array(moment_share, PROBES, ROWS), array(moment_share, PROBES, PROBES)),
        [SMEM] * 3 + [VMEM] * 11 + [HBM] * 2,
        vmem=24,
        scratch=[pltpu.VMEM((DEGREE + 1, PROBES, ROWS), f32), pltpu.SemaphoreType.DMA((DEGREE + 1,))],
    )(node, flag, jnp.asarray(moment_weights()), *early, *late, direction, dir_against, *state, probes, kept)
    return (moments, projected)


def solution(mesh):
    placed = (P(None, "row"), P("row", None, None), P("row", None, None, None), P("row", None))
    return jax.shard_map(
        shards,
        mesh=mesh,
        in_specs=placed,
        out_specs=(P("node", None, "row"), P("node", None, None)),
        check_vma=False,
    )
```

```python
import functools
import math

import jax
import jax.numpy as jnp
import numpy as np
from jax import lax
from jax.experimental import pallas as pl
from jax.experimental.pallas import tpu as pltpu
from jax.sharding import PartitionSpec as P

NODES = 8
MOMENTS = 16
REACH = 4
ITERS = 4
PROBES = 32
BLOCK = 128
ROWS = 1024
HALF = 512
TILE = 256
DEGREE = 2 * ITERS - 1
BLOCKS = 512
ORDER_DIM = BLOCKS * BLOCK
SCALE = 16.0

f32 = jnp.float32
bf16 = jnp.bfloat16
highest = lax.Precision.HIGHEST

TILES = [(row, col) for row in range(4) for col in range(row, min(row + 3, 4))]
EDGE = [(row, col) for row in range(REACH) for col in range(row + 1)]

VMEM = pl.BlockSpec(memory_space=pltpu.VMEM)
SMEM = pl.BlockSpec(memory_space=pltpu.SMEM)


HBM = pl.BlockSpec(memory_space=pltpu.HBM)


def call(body, outs, in_specs, flops=0, bytes_accessed=0, vmem=8, scratch=(), out_specs=None, aliases=()):
    return pl.pallas_call(
        body,
        out_shape=outs,
        in_specs=in_specs,
        out_specs=jax.tree.map(lambda _: VMEM, outs) if out_specs is None else out_specs,
        input_output_aliases=dict(aliases),
        scratch_shapes=scratch,
        compiler_params=pltpu.CompilerParams(vmem_limit_bytes=vmem << 20),
        cost_estimate=pl.CostEstimate(flops=flops, bytes_accessed=bytes_accessed, transcendentals=0),
    )


def halves(value):
    high = value.astype(bf16)
    return high, (value - high.astype(f32)).astype(bf16)


def stacked(value):
    high, low = halves(value)
    return jnp.concatenate([high, low], axis=0)


def dot_nn(left, right):
    return lax.dot_general(left, right, (((1,), (0,)), ((), ())), preferred_element_type=f32)


def dot_nt(left, right):
    return lax.dot_general(left, right, (((1,), (1,)), ((), ())), preferred_element_type=f32)


def fold(double):
    half = double.shape[0] // 2
    return double[:half] + double[half:]


def product(dot, pair, high, low):
    return fold(dot(pair, high)) + dot(pair[:pair.shape[0] // 2], low)


def payloads(parity, near, spill, pay_core, pay_chip):
    even = parity == 0
    pay_core[...] = jnp.where(even, spill, near)
    pay_chip[...] = jnp.where(even, near, spill)


def cross_out(tail, uhi, ulo):
    pair = stacked(tail)
    left, right = pair[:, :TILE], pair[:, TILE:]
    first = product(dot_nn, left, uhi[0], ulo[0]) + product(dot_nn, right, uhi[1], ulo[1])
    return jnp.concatenate([first, product(dot_nn, right, uhi[2], ulo[2])], axis=1)


def cross_in(ahead, uhi, ulo):
    pair = stacked(ahead)
    left, right = pair[:, :TILE], pair[:, TILE:]
    second = product(dot_nt, left, uhi[1], ulo[1]) + product(dot_nt, right, uhi[2], ulo[2])
    return jnp.concatenate([product(dot_nt, left, uhi[0], ulo[0]), second], axis=1)


def band_block(step, row, neighbours, position, diag, coup):
    if step == 0:
        return diag * (0.5 / SCALE)
    block = jnp.zeros((BLOCK, BLOCK), f32)
    for f in range(neighbours.shape[0]):
        distance = (neighbours[f, row] - (position * 8 + row)) & (BLOCKS - 1)
        block = block + jnp.where(distance == step, coup[f], 0.0)
    return block * (1.0 / SCALE)


def cross_place(row, col):
    return row // 2 + col // 2, pl.ds(row % 2 * BLOCK, BLOCK), pl.ds(col % 2 * BLOCK, BLOCK)


def cross_zero(uhi, ulo):
    zero = jnp.zeros((BLOCK, BLOCK), bf16)
    for row, col in ((0, 1), (2, 3)):
        uhi[cross_place(row, col)] = zero
        ulo[cross_place(row, col)] = zero


def cross_rows(i, neighbours, position, coup, uhi, ulo, edge=None):
    row = i - 4
    for col in range(row + 1):
        block = band_block(8 + col - i, i, neighbours, position, None, coup)
        uhi[cross_place(row, col)], ulo[cross_place(row, col)] = halves(block)
        if edge is not None:
            edge[EDGE.index((row, col))] = block


def cross_body(neighbours, position, coup_hbm, x_hbm, pay_core, pay_chip, coup, x, uhi, ulo, sems):
    copies = [pltpu.make_async_copy(coup_hbm.at[i], coup.at[i - 4], sems.at[i - 4]) for i in (7, 6, 5, 4)]
    for copy in copies:
        copy.start()
    load = pltpu.make_async_copy(x_hbm, x, sems.at[4])
    load.start()
    cross_zero(uhi, ulo)
    for i, copy in zip((7, 6, 5, 4), copies):
        copy.wait()
        cross_rows(i, neighbours, position[0], coup.at[i - 4], uhi, ulo)
    load.wait()
    payloads(position[0] & 1, x[:, :HALF], cross_out(x[:, HALF:], uhi, ulo), pay_core, pay_chip)


def gram_of(x, before):
    both = jnp.concatenate([before, x], axis=0)
    return lax.dot_general(x, both, (((1,), (1,)), ((), ())), precision=highest, preferred_element_type=f32)


def first_body(neighbours, position, diag, coup, x, after, thi, tlo, uhi, ulo, edge, local, gram):
    zero = jnp.zeros((BLOCK, BLOCK), bf16)
    for tile, (row, col) in enumerate(TILES):
        for up in range(2):
            for across in range(2):
                i, step = 2 * row + up, 2 * (col - row) + across - up
                at = tile, pl.ds(up * BLOCK, BLOCK), pl.ds(across * BLOCK, BLOCK)
                if 0 <= step <= REACH:
                    block = band_block(step, i, neighbours, position[0], diag[i] if step == 0 else None, coup.at[i])
                    thi[at], tlo[at] = halves(block)
                else:
                    thi[at] = zero
                    tlo[at] = zero
    cross_zero(uhi, ulo)
    for i in range(4, 8):
        cross_rows(i, neighbours, position[0], coup.at[i], uhi, ulo, edge)
    value = x[...]
    local[...] = times_local(value, thi, tlo)
    gram[...] = gram_of(value, value)


def times_local(value, thi, tlo):
    pair = stacked(value)
    wide = [jnp.zeros((2 * PROBES, TILE), f32) for _ in range(4)]
    thin = [jnp.zeros((PROBES, TILE), f32) for _ in range(4)]
    for tile, (row, col) in enumerate(TILES):
        high, low = thi[tile], tlo[tile]
        from_row, from_col = pair[:, row * TILE:(row + 1) * TILE], pair[:, col * TILE:(col + 1) * TILE]
        wide[col] = wide[col] + dot_nn(from_row, high)
        thin[col] = thin[col] + dot_nn(from_row[:PROBES], low)
        wide[row] = wide[row] + dot_nt(from_col, high)
        thin[row] = thin[row] + dot_nt(from_col[:PROBES], low)
    return jnp.concatenate([fold(w) + t for w, t in zip(wide, thin)], axis=1)


def joined(local, arrived, inward):
    return jnp.concatenate([local[:, :HALF] + arrived, local[:, HALF:] + inward], axis=1)


def send_two(position, value, thi, tlo, uhi, ulo, local, spill, pay_core, pay_chip):
    following = times_local(value, thi, tlo)
    local[...] = following
    both = cross_out(jnp.concatenate([value[:, HALF:], following[:, HALF:]], axis=0), uhi, ulo)
    spill[...] = both[:PROBES]
    near = jnp.concatenate([value[:, :HALF], following[:, :HALF]], axis=0)
    payloads(position[0] & 1, near, both, pay_core, pay_chip)


def received(position, got_core, got_chip):
    even = position[0] & 1 == 0
    core, chip = got_core[...], got_chip[...]
    return jnp.where(even, core, chip), jnp.where(even, chip, core)


def start_body(position, local, got_core, got_chip, thi, tlo, uhi, ulo, kept, out, *rest):
    *sent, sems = rest
    ahead, arrived = received(position, got_core, got_chip)
    value = joined(local, arrived, cross_in(ahead, uhi, ulo))
    out[...] = value
    keep = pltpu.make_async_copy(out, kept.at[1], sems.at[0])
    keep.start()
    send_two(position, value, thi, tlo, uhi, ulo, *sent)
    keep.wait()


def double_body(
    kept_in, position, before, local, spill, correction, got_core, got_chip, thi, tlo, uhi, ulo, kept, first, second, *rest,
    degree
):
    *sent, sems = rest
    ahead, arrived = received(position, got_core, got_chip)
    ahead = jnp.concatenate([ahead[:PROBES], ahead[PROBES:] + spill[...]], axis=0)
    inward = cross_in(ahead, uhi, ulo)
    value = joined(local, arrived[:PROBES], inward[:PROBES])
    first[...] = value
    keeps = [pltpu.make_async_copy(ref, kept.at[degree + 1 + n], sems.at[n]) for n, ref in enumerate((first, second))]
    keeps[0].start()
    local = times_local(value, thi, tlo)
    after = joined(local, arrived[PROBES:] + correction[...], inward[PROBES:])
    second[...] = after
    keeps[1].start()
    if len(sent) > 2:
        send_two(position, after, thi, tlo, uhi, ulo, *sent)
    else:
        sums = jnp.concatenate([gram_of(value, before[...]), gram_of(after, value)], axis=1)
        store_halves(position, sums, *sent)
    for keep in keeps:
        keep.wait()


def store_halves(position, sums, mine, other):
    upper, lower = sums[:PROBES // 2], sums[PROBES // 2:]
    even = position[0] & 1 == 0
    mine[...] = jnp.where(even, upper, lower)
    other[...] = jnp.where(even, lower, upper)


def shadow_body(position, *refs, count, first, last):
    vectors, (done, up_hi, up_lo), outs = refs[:count], refs[count:count + 3], refs[count + 3:]
    correction, outs = outs[0], outs[1:]
    if first:
        phi, plo = outs[1:]
        cross_zero(phi, plo)
        for n, (row, col) in enumerate(EDGE):
            phi[cross_place(row, col)], plo[cross_place(row, col)] = halves(up_hi[n])
    else:
        phi, plo = up_hi, up_lo
    sums = [done[...]] + [gram_of(vectors[n][...], vectors[n - 1][...]) for n in range(1, count)]
    sums = jnp.concatenate(sums, axis=1)
    if last:
        store_halves(position, sums, *outs)
    else:
        outs[0][...] = sums
    correction[...] = cross_out(cross_in(vectors[-1][:, :HALF], phi, plo), phi, plo)


def dot_f32(left, right):
    return lax.dot_general(left, right, (((1,), (0,)), ((), ())), precision=highest, preferred_element_type=f32)


WIDTH = NODES * PROBES
PANEL = 8


def invert(matrix):
    rows = lax.broadcasted_iota(jnp.int32, (PROBES, WIDTH), 0)
    lanes = lax.broadcasted_iota(jnp.int32, (PROBES, WIDTH), 1) % PROBES
    group = lax.broadcasted_iota(jnp.int32, (PROBES, BLOCK), 1) // PROBES * PROBES
    for start in range(0, PROBES, PANEL):
        columns = [
            jnp.concatenate(
                [jnp.take_along_axis(matrix[:, h:h + BLOCK], group + k, axis=1) for h in range(0, WIDTH, BLOCK)], axis=1
            )
            for k in range(start, start + PANEL)
        ]
        for m in range(PANEL):
            k = start + m
            on_row, on_lane = rows == k, lanes == k
            inverse = 1.0 / columns[m][k:k + 1]
            factor = jnp.where(on_row, -1.0, columns[m])
            scaled = jnp.where(on_lane[:1], 1.0, matrix[k:k + 1]) * inverse
            matrix = jnp.where(on_lane | on_row, 0.0, matrix) - factor * scaled
            for q in range(m + 1, PANEL):
                columns[q] = jnp.where(on_row, 0.0, columns[q]) - factor * (columns[q][k:k + 1] * inverse)
    return matrix


def node_diagonal():
    return (
        lax.broadcasted_iota(jnp.int32, (WIDTH, WIDTH), 0) // PROBES
        == lax.broadcasted_iota(jnp.int32, (WIDTH, WIDTH), 1) // PROBES
    )


def node_shifts():
    node = lax.broadcasted_iota(jnp.int32, (1, WIDTH), 1) // PROBES
    cosine = jnp.zeros((1, WIDTH), f32)
    square = jnp.zeros((1, WIDTH), f32)
    for j in range(NODES):
        angle = math.pi * (j + 0.5) / NODES
        cosine = jnp.where(node == j, np.float32(math.cos(angle)), cosine)
        square = jnp.where(node == j, np.float32(math.sin(angle) ** 2), square)
    return cosine, square


def grown(coeffs, blocks=1):
    return jnp.concatenate([coeffs, jnp.zeros((blocks * PROBES, WIDTH), f32)], axis=0)


def sunk(coeffs, cosine):
    below = jnp.concatenate([jnp.zeros((PROBES, WIDTH), f32), coeffs], axis=0)
    return SCALE * below - cosine * grown(coeffs)


def raised(against, cosine):
    return SCALE * against[PROBES:] - cosine * against[:-PROBES]


class Nodes:
    def __init__(self):
        self.diagonal = node_diagonal()
        self.cosine, self.square = node_shifts()

    def blocks(self, full):
        masked = jnp.where(self.diagonal, full, 0.0)
        return sum(masked[j * PROBES:(j + 1) * PROBES] for j in range(NODES))

    def spread(self, matrix):
        return jnp.where(self.diagonal, jnp.concatenate([matrix] * NODES, axis=0), 0.0)

    def inner(self, left, against):
        return self.blocks(dot_f32(left.T, against[:left.shape[0]]))

    def image(self, direction, dir_against):
        once, once_against = sunk(direction, self.cosine), raised(dir_against, self.cosine)
        image = sunk(once, self.cosine) + self.square * grown(direction, 2)
        image_against = raised(once_against, self.cosine) + self.square * dir_against[:-2 * PROBES]
        return image, image_against

    def alpha(self, direction, residual, dir_against, res_against, solution):
        size = direction.shape[0]
        image, image_against = self.image(direction, dir_against)
        if size == PROBES:
            curvature, now = image_against[:size], res_against[:size]
        else:
            turned = direction.T
            curvature = self.blocks(dot_f32(turned, image_against[:size]))
            now = self.blocks(dot_f32(turned, res_against[:size]))
        inverse = invert(curvature)
        alpha = self.spread(dot_f32(inverse, self.spread(now)))
        if residual is None:
            return grown(solution, 2) + dot_f32(direction, alpha)
        moved = dot_f32(jnp.concatenate([direction, image, image_against], axis=0), alpha)
        part = size + image.shape[0]
        solution = moved[:size] if solution is None else grown(solution, 2) + moved[:size]
        residual = grown(residual, 2) - moved[size:part]
        res_against = res_against[:-2 * PROBES] - moved[part:]
        return image, inverse, residual, res_against, solution

    def beta(self, direction, dir_against, image, inverse, residual, res_against):
        size, count = direction.shape[0], res_against.shape[0]
        beta = self.spread(dot_f32(inverse, self.spread(self.inner(image, res_against))))
        moved = dot_f32(jnp.concatenate([direction, dir_against[:count]], axis=0), beta)
        return residual - grown(moved[:size], 2), res_against - moved[size:]


def moment_coeffs(nodes, weights, first, share, solution):
    applied = sunk(solution, nodes.cosine)
    row = lax.broadcasted_iota(jnp.int32, (PROBES, share * PROBES), 0)
    lane = lax.broadcasted_iota(jnp.int32, (PROBES, share * PROBES), 1)
    imag, real = [], []
    for j in range(NODES):
        for part, (table, sign) in ((imag, (0, 1.0)), (real, (1, -1.0))):
            block = jnp.zeros((PROBES, share * PROBES), f32)
            for k in range(share):
                block = jnp.where(lane == row + k * PROBES, sign * weights[table, first + k, j], block)
            part.append(block)
    left = jnp.concatenate([grown(solution), applied], axis=1)
    return dot_f32(left, jnp.concatenate(imag + real, axis=0))


def whole(position, mine, other):
    even = position[0] & 1 == 0
    upper, lower = jnp.where(even, mine[...], other[...]), jnp.where(even, other[...], mine[...])
    return jnp.concatenate([upper, lower], axis=0)


def store(outs, values):
    for out, value in zip(outs, values):
        out[...] = value


def zeroth_body(position, mine, other, *outs):
    nodes = Nodes()
    sums = whole(position, mine, other)
    against = jnp.concatenate(
        [
            jnp.concatenate([sums[:, at:at + PROBES]] * NODES, axis=1)
            for at in range(PROBES, sums.shape[1], PROBES)
        ],
        axis=0,
    )
    eye = (
        lax.broadcasted_iota(jnp.int32, (PROBES, WIDTH), 0)
        == lax.broadcasted_iota(jnp.int32, (PROBES, WIDTH), 1) % PROBES
    ).astype(f32)
    image, inverse, residual, res_against, solution = nodes.alpha(eye, eye, against, against, None)
    direction, dir_against = nodes.beta(eye, against, image, inverse, residual, res_against)
    store(outs, (direction, residual, dir_against, res_against, solution))


def iterate_body(*refs):
    nodes = Nodes()
    direction, residual, dir_against, res_against, solution = (ref[...] for ref in refs[:5])
    image, inverse, residual, res_against, solution = nodes.alpha(
        direction, residual, dir_against, res_against, solution
    )
    direction, dir_against = nodes.beta(direction, dir_against, image, inverse, residual, res_against)
    store(refs[5:], (direction, residual, dir_against, res_against, solution))


def alpha_body(*refs):
    store(refs[5:], Nodes().alpha(*(ref[...] for ref in refs[:5])))


def moments_body(
    node, position, weights, mine, other, mine_late, other_late, direction, dir_against,
    image, inverse, residual, res_against, solution, k0, kept, moments, projected, basis, sems
):
    loads = [pltpu.make_async_copy(k0, basis.at[0], sems.at[0])]
    loads += [pltpu.make_async_copy(kept.at[d], basis.at[d], sems.at[d]) for d in range(1, DEGREE + 1)]
    for load in loads:
        load.start()
    nodes = Nodes()
    sums = jnp.concatenate([whole(position, mine, other)[:, PROBES:], whole(position, mine_late, other_late)], axis=1)

    def against(coeffs, old):
        size = coeffs.shape[0]
        rows = [sums[:, a:a + size] for a in range(old.shape[0], (DEGREE + 2) * PROBES, PROBES)]
        return jnp.concatenate([old, dot_f32(jnp.concatenate(rows, axis=0), coeffs)], axis=0)

    direction, residual = direction[...], residual[...]
    res_against = against(residual, res_against[...])
    dir_against = against(direction, dir_against[...])
    direction, dir_against = nodes.beta(direction, dir_against, image[...], inverse[...], residual, res_against)
    result = nodes.alpha(direction, None, dir_against, res_against, solution[...])
    share = moments.shape[0]
    coeffs = moment_coeffs(nodes, weights, node[0] * share, share, result)
    onto = dot_f32(sums[:, :PROBES * (DEGREE + 1)], coeffs) * (1.0 / ORDER_DIM)
    for k in range(share):
        projected[k] = onto[:, k * PROBES:(k + 1) * PROBES]
    turned = coeffs.T
    for load in loads:
        load.wait()
    moments[...] = dot_f32(turned, basis[...].reshape((DEGREE + 1) * PROBES, ROWS)).reshape(share, PROBES, ROWS)


def add_body(left, right, out):
    out[...] = left[...] + right[...]


def pack_body(early, early_got, late, late_got, out):
    lanes = early.shape[1]
    out[:, :lanes] = early[...] + early_got[...]
    out[:, lanes:] = late[...] + late_got[...]


def exchange(value, partner):
    count = lax.axis_size("row")
    return lax.ppermute(value, "row", [(source, partner(source) % count) for source in range(count)])


def core_partner(i):
    return i ^ 1


def chip_partner(i):
    return i + 1 if i % 2 else i - 1


def ring_partner(stage, i):
    y, z, core = i // 16, i // 2 % 8, i % 2
    if stage < 3:
        z = (z ^ 1, z ^ 2, (6, 7, 4, 5, 2, 3, 0, 1)[z])[stage]
    else:
        y = (y ^ 1, y ^ 3)[stage - 3]
    return y * 16 + z * 2 + core


def add(left, right):
    return call(add_body, jax.ShapeDtypeStruct(left.shape, f32), [VMEM] * 2, vmem=4)(left, right)


def stage(value, number):
    return add(value, exchange(value, functools.partial(ring_partner, number)))


def moment_weights():
    orders = np.arange(MOMENTS)[:, None] + 1.0
    angles = np.pi * (np.arange(NODES)[None, :] + 0.5) / NODES
    imag = np.sin(orders * angles) * np.sin(angles) / 8.0
    real = np.cos(orders * angles) / 8.0
    return np.stack([imag, real]).astype(np.float32)


def shards(probes, diag_blocks, couplings, neighbours):
    moment_share = MOMENTS // lax.axis_size("node")
    position = lax.axis_index("row")
    flag = position.reshape(1)
    node = lax.axis_index("node").reshape(1)
    near_by = neighbours.T
    def array(*shape, kind=f32):
        return jax.ShapeDtypeStruct(shape, kind)

    message = array(PROBES, HALF)
    vector = array(PROBES, ROWS)
    pair = array(PROBES, 2 * PROBES)
    double = array(2 * PROBES, HALF)
    band = (array(len(TILES), TILE, TILE, kind=bf16),) * 2
    cross = (array(3, TILE, TILE, kind=bf16),) * 2
    stack = array(DEGREE + 1, PROBES, ROWS)
    copies = pltpu.SemaphoreType.DMA((2,))
    pay_core, pay_chip = call(
        cross_body,
        (message, message),
        [SMEM, SMEM, HBM, HBM],
        vmem=56,
        scratch=[
            pltpu.VMEM((4, 3, BLOCK, BLOCK), f32),
            pltpu.VMEM((PROBES, ROWS), f32),
            pltpu.VMEM((3, TILE, TILE), bf16),
            pltpu.VMEM((3, TILE, TILE), bf16),
            pltpu.SemaphoreType.DMA((5,)),
        ],
    )(near_by, flag, couplings, probes)
    got_core = exchange(pay_core, core_partner)
    got_chip = exchange(pay_chip, chip_partner)
    thi, tlo, uhi, ulo, edge, local, gram = call(
        first_body,
        band + cross + (array(len(EDGE), BLOCK, BLOCK), vector, pair),
        [SMEM, SMEM, VMEM, VMEM, VMEM, HBM],
        flops=10**9,
        bytes_accessed=4 << 20,
        vmem=16,
    )(near_by, flag, diag_blocks, couplings, probes, got_core)
    edge, got_chip = lax.optimization_barrier((edge, got_chip))
    edge = exchange(edge, lambda i: i + 1)
    blocks = (thi, tlo, uhi, ulo)
    sent = (vector, message, double, double)
    kept, value, local, spill, pay_core, pay_chip = call(
        start_body,
        (stack, vector) + sent,
        [SMEM] + [VMEM] * 7,
        flops=10**9,
        bytes_accessed=4 << 20,
        out_specs=(HBM,) + (VMEM,) * 5,
        scratch=[copies],
    )(flag, local, got_core, got_chip, *blocks)
    fresh = [probes, value]
    previous = (edge, edge)
    for degree in range(1, DEGREE, 2):
        got_core = exchange(pay_core, core_partner)
        got_chip = exchange(pay_chip, chip_partner)
        more = degree + 2 < DEGREE
        first = degree == 1
        lanes = gram.shape[1] + 2 * PROBES * (len(fresh) - 1)
        sums = (array(PROBES, lanes),) if more else (array(PROBES // 2, lanes),) * 2
        correction, *made = call(
            functools.partial(shadow_body, count=len(fresh), first=first, last=not more),
            (message,) + sums + (cross if first else ()),
            [SMEM] + [VMEM] * (len(fresh) + 3),
            flops=10**9,
            bytes_accessed=2 << 20,
        )(flag, *fresh, gram, *previous)
        if first:
            previous = made[1:]
        if more:
            gram = made[0]
        else:
            early = stage(add(made[0], exchange(made[1], core_partner)), 0)
            early, got_core, got_chip = lax.optimization_barrier((early, got_core, got_chip))
            arrived = exchange(early, functools.partial(ring_partner, 3))
        outs = (stack, vector, vector) + (sent if more else (array(PROBES // 2, 4 * PROBES),) * 2)
        kept, value, after, *rest = call(
            functools.partial(double_body, degree=degree),
            outs,
            [HBM, SMEM] + [VMEM] * 10,
            flops=10**9,
            bytes_accessed=4 << 20,
            out_specs=(HBM,) + (VMEM,) * (len(outs) - 1),
            scratch=[copies],
            aliases=((0, 0),),
        )(kept, flag, fresh[-1], local, spill, correction, got_core, got_chip, *blocks)
        fresh = [fresh[-1], value, after]
        if more:
            local, spill, pay_core, pay_chip = rest
    late, other, arrived = lax.optimization_barrier((*rest, arrived))
    early = add(early, arrived)

    def coeffs(blocks):
        return array(blocks * PROBES, WIDTH)

    work = dict(flops=3 * 10**9, bytes_accessed=4 << 20, vmem=16)
    lanes = early.shape[1]
    pack = call(pack_body, array(PROBES // 2, lanes + late.shape[1]), [VMEM] * 4, vmem=4)(
        early, exchange(early, functools.partial(ring_partner, 1)), late, exchange(other, core_partner)
    )
    pack = stage(stage(pack, 2), 4)
    early, late = pack[:, :lanes], pack[:, lanes:]

    def beside(number, body, blocks, specs, *args):
        got = exchange(late, functools.partial(ring_partner, number))
        made = call(body, tuple(map(coeffs, blocks)), specs, **work)(*args)
        got, made = lax.optimization_barrier((got, made))
        return add(late, got), made

    early = (early, exchange(early, core_partner))
    late, state = beside(3, zeroth_body, (3, 3, 9, 9, 1), [SMEM, VMEM, VMEM], flag, *early)
    late, state = beside(1, iterate_body, (5, 5, 7, 7, 3), [VMEM] * 5, *state)
    direction, _, dir_against, _, _ = state
    late, state = beside(0, alpha_body, (7, 1, 7, 5, 5), [VMEM] * 5, *state)
    late = (late, exchange(late, core_partner))
    moments, projected = call(
        moments_body,
        (array(moment_share, PROBES, ROWS), array(moment_share, PROBES, PROBES)),
        [SMEM] * 3 + [VMEM] * 11 + [HBM] * 2,
        vmem=24,
        scratch=[pltpu.VMEM((DEGREE + 1, PROBES, ROWS), f32), pltpu.SemaphoreType.DMA((DEGREE + 1,))],
    )(node, flag, jnp.asarray(moment_weights()), *early, *late, direction, dir_against, *state, probes, kept)
    return (moments, projected)


def solution(mesh):
    placed = (P(None, "row"), P("row", None, None), P("row", None, None, None), P("row", None))
    return jax.shard_map(
        shards,
        mesh=mesh,
        in_specs=placed,
        out_specs=(P("node", None, "row"), P("node", None, None)),
        check_vma=False,
    )
```
